128 devices in a mesh: space: 8 (over x, y_lo), tm: 16 (over y_hi, z, core).
Axes of the slice: x: 4, y: 4 (y_hi: 2, y_lo: 2; y = y_hi * 2 + y_lo), z: 4, core: 2. Of those that a mesh axis runs over, the one named last changes fastest.
Arguments:
- snapshots: bfloat16 [24576, 4096], P('space', 'tm'), may hold values from -6 to 6
- coefficients: bfloat16 [4096, 64], replicated, may hold values from -0.09375 to 0.09375
Outputs:
- gram: float32 [4096, 4096], P('space', 'tm')
- modes: bfloat16 [24576, 64], P('space')
- amplitudes: float32 [4096, 64], P('tm')
- residual: bfloat16 [24576, 4096], P('space', 'tm')
The draws below stay inside these ranges and needn't reach their ends.
All inputs are finite; a program needn't handle non-finite values.
Results may differ from the reference program's by a relative error of at most 0.0034.
Values may be sent and summed in bfloat16 or wider, within the bound.
A program may use at most 128 MiB of HBM per device.

```python
import jax
import jax.numpy as jnp
from jax import lax

RANK = 64
CELLS = 24576
SNAPS = 4096


def steps_of(key, dims, shards, smallest, largest):
    loudness, own = 1.0, jax.random.fold_in(key, 6)
    for axis_at, blocks in shards:
        steps = jnp.exp(jax.random.uniform(jax.random.fold_in(own, axis_at), (blocks,), jnp.float32, smallest / len(shards), largest / len(shards)))
        loudness = loudness * jnp.repeat(steps, dims[axis_at] // blocks).reshape([-1 if axis == axis_at else 1 for axis in range(len(dims))])
    return loudness


def gaussian(stream_key, shape, width, reach, split=(), kind=jnp.bfloat16):
    level = steps_of(stream_key, shape, split, -0.22, 0.18) if split else 1.0
    values = jax.random.normal(stream_key, shape, jnp.float32) * width * level
    return jnp.minimum(jnp.maximum(values, -reach), reach).astype(kind)


def setup_inputs(seed: int = 0) -> dict:
    key_of = jax.random.split(jax.random.key(seed), 3)
    snapshots = gaussian(key_of[0], (CELLS, SNAPS), 1.0, 6.0, ((0, 8), (1, 16)))
    coefficients = gaussian(key_of[1], (SNAPS, RANK), SNAPS ** -0.5, 0.09375)
    return dict(snapshots=snapshots, coefficients=coefficients)


def reference(snapshots, coefficients):
    gram = lax.dot_general(snapshots, snapshots, (((0,), (0,)), ((), ())), preferred_element_type=jnp.float32) / CELLS
    coeff_full = coefficients.astype(jnp.float32)
    weighted = jnp.dot(gram, coeff_full, precision=lax.Precision.HIGHEST)
    projected = jnp.dot(snapshots, coefficients, preferred_element_type=jnp.float32)
    energy = lax.optimization_barrier(jnp.sum(coeff_full * weighted, axis=0))
    scale = lax.rsqrt(energy)
    modes = (projected * scale[None, :]).astype(jnp.bfloat16)
    amplitudes = jnp.sqrt(jnp.float32(CELLS)) * weighted * scale[None, :]
    slow_part = jnp.dot(modes.astype(jnp.float32), amplitudes.T, precision=lax.Precision.HIGHEST)
    residual = (snapshots.astype(jnp.float32) - slow_part / jnp.sqrt(jnp.float32(CELLS))).astype(jnp.bfloat16)
    return (gram, modes, amplitudes, residual)
```

```python
import jax
import jax.numpy as jnp
from jax import lax
from jax.experimental import pallas as pl
from jax.experimental.pallas import tpu as pltpu
from jax.sharding import PartitionSpec as P

MESH = pl.DeviceIdType.MESH
F32, BF16 = jnp.float32, jnp.bfloat16
CHUNKS = 4


def device_at(x, y, z, c):
    x, y, z = x % 4, y % 4, z % 4
    return (x * 2 + y % 2, (y // 2) * 8 + z * 2 + c)


def wait_for(ref, sem):
    pltpu.make_async_copy(ref, ref, sem).wait()


def split(value):
    high = value.astype(BF16)
    return high, (value - high.astype(F32)).astype(BF16)


def kernel(
    snaps, coeffs, gram, modes, amps, resid,
    own, coef, base, north, south, cross, line_x, sum_x, line_y, mirror, direct, flipped, flip_in,
    part, sib_part, pieces, proj, weight, weights,
    local_sem, y_send, y_recv, sib_send, sib_recv, n_send, n_recv, m_send, m_recv, ms_send, ms_recv,
    x_send, x_recv, l_send, l_recv, d_send, d_recv, t_send, t_recv,
    p_send, p_recv, r_send, r_recv, g_send, g_recv, f_send, f_recv, w_send, w_recv,
):
    space, tm = lax.axis_index("space"), lax.axis_index("tm")
    x, yl, yh, z, c = space // 2, space % 2, tm // 8, (tm // 2) % 4, tm % 2
    y, chip, oh, oc = 2 * yh + yl, tm // 2, 1 - yh, 1 - c
    cells, cols = own.shape
    half, quarter, step = cells // 2, cells // 4, cells // 2 // CHUNKS
    total_cells = cells * 8
    rank = coef.shape[0]
    row_at = 2 * (x % 2) + yl
    role = (row_at - z + 4) % 4
    zs = (z, z, (z + 3) % 4)
    pending = []

    def copy(src, dst, send, recv, device, when=None):
        remote = pltpu.make_async_remote_copy(
            src_ref=src, dst_ref=dst, send_sem=send, recv_sem=recv, device_id=device, device_id_type=MESH
        )
        if when is None:
            remote.start()
        else:
            pl.when(when)(remote.start)
        pending.append((remote, when))

    sibling = device_at(x, y, z, oc)
    partner = device_at(x, y + 2, z, c)
    below, above = device_at(x, y, z + 3, c), device_at(x, y, z + 1, c)

    def turned(at_x, at_y, at_z):
        return 2 * (at_y // 2) + (at_z % 4) // 2, 2 * (at_x // 2) + at_z % 2

    barrier = pltpu.get_barrier_semaphore()

    def greet(device, when=None):
        def do():
            pl.semaphore_signal(barrier, inc=1, device_id=device, device_id_type=MESH)

        do() if when is None else pl.when(when)(do)

    sends = (role == 0) | (role == 3)
    greet(sibling)
    greet(device_at(x, 2 * oh + 1 - yl, z, c))
    for k in range(1, 8):
        greet((space, ((chip + k) % 8) * 2 + c))
        greet(((space + k) % 8, tm))
    from_x, from_y = turned(x, y, z)
    from_z = jnp.where(role == 1, z, z + 1)
    for k in range(2):
        greet(device_at(from_x, from_y, from_z, k), (role == 1) | (role == 2))
    pl.semaphore_wait(barrier, jnp.where(sends, 18, 16))

    keep = pl.ds(pl.multiple_of(yh * half, half), half)
    mine = pltpu.make_async_copy(snaps.at[keep], base.at[yh, c], local_sem.at[0])
    mine.start()
    whole = pltpu.make_async_copy(snaps, own, local_sem.at[1])
    whole.start()
    coef_own = pltpu.make_async_copy(
        coeffs.at[:, pl.ds(pl.multiple_of(tm * cols, cols), cols)], coef, local_sem.at[2]
    )
    coef_own.start()

    for k in range(CHUNKS):
        rows = pl.ds(pl.multiple_of(oh * half + k * step, step), step)
        copy(snaps.at[rows], base.at[yh, c, pl.ds(k * step, step)], y_send.at[k], y_recv.at[k], partner)
    copy(snaps.at[keep], base.at[yh, c], sib_send.at[0], sib_recv.at[0], sibling)
    copy(snaps.at[keep], north.at[yh], n_send.at[0], n_recv.at[0], below)
    piece_for = ((z + 1) % 4) // 2
    rows = pl.ds(pl.multiple_of(yh * half + piece_for * quarter, quarter), quarter)
    copy(snaps.at[rows], south.at[yh, c], m_send.at[0], m_recv.at[0], above)

    coef_own.wait()
    whole.wait()

    @pl.loop(0, 4)
    def _(k):
        at = pl.ds(pl.multiple_of(k * (cells // 4), cells // 4), cells // 4)
        part[:, at] = lax.dot_general(
            coef[...], own[at, :], (((1,), (1,)), ((), ())), preferred_element_type=F32
        )

    other_half = pl.ds(pl.multiple_of(oc * half, half), half)
    copy(part.at[:, other_half], sib_part, p_send, p_recv, sibling)
    wait_for(sib_part, p_recv)
    own_half = pl.ds(pl.multiple_of(c * half, half), half)
    sib_part[...] += part[:, own_half]
    for k in range(1, 8):
        to = (chip + k) % 8
        rows = pl.ds(pl.multiple_of(to * 8, 8), 8)
        copy(sib_part.at[rows], pieces.at[k - 1], r_send.at[k - 1], r_recv.at[k - 1], (space, to * 2 + c))

    def relay(k):
        rows = pl.ds(k * step, step)
        wait_for(base.at[oh, c, rows], y_recv.at[k])
        src = base.at[oh, c, rows]
        copy(src, base.at[oh, c, rows], sib_send.at[1 + k], sib_recv.at[1 + k], sibling)
        copy(src, north.at[oh, rows], n_send.at[1 + k], n_recv.at[1 + k], below)
        inside = pl.ds((k % 2) * step, step)
        copy(
            src, south.at[oh, c, inside], m_send.at[1 + k % 2], m_recv.at[1 + k % 2], above, piece_for == k // 2
        )

    relay(0)

    for k in range(7):
        wait_for(pieces.at[k], r_recv.at[k])
    rows8 = pl.ds(pl.multiple_of(chip * 8, 8), 8)
    piece = sib_part[rows8, :]
    for k in range(7):
        piece = piece + pieces[k]
    proj[c, rows8, :] = piece
    for k in range(1, 8):
        to = (chip + k) % 8
        copy(proj.at[c, rows8], proj.at[c, rows8], g_send.at[k - 1], g_recv.at[k - 1], (space, to * 2 + c))

    relay(1)

    for k in range(1, 8):
        rows = pl.ds(pl.multiple_of(((chip - k + 8) % 8) * 8, 8), 8)
        wait_for(proj.at[c, rows], g_recv.at[k - 1])
    copy(proj.at[c], proj.at[c], f_send, f_recv, sibling)
    wait_for(proj.at[oc], f_recv)

    relay(2)

    sums = jnp.zeros((rank, cols), F32)
    squares = jnp.zeros((rank, 1), F32)
    for k in range(2):
        value = proj[k]
        squares = squares + jnp.sum(value * value, axis=1, keepdims=True)
        high, low = split(value)
        block = own[k * half : (k + 1) * half, :]
        sums = sums + jnp.dot(high, block, preferred_element_type=F32)
        sums = sums + jnp.dot(low, block, preferred_element_type=F32)
    weight[:, :cols] = sums
    weight[:, cols:] = jnp.broadcast_to(squares, (rank, 128))
    for k in range(1, 8):
        copy(weight, weights.at[k - 1], w_send.at[k - 1], w_recv.at[k - 1], ((space + k) % 8, tm))

    relay(3)
    mine.wait()

    wait_for(south.at[yh, c], m_recv.at[0])
    copy(south.at[yh, c], south.at[yh, c], ms_send.at[0], ms_recv.at[0], sibling)

    wait_for(base.at[yh, oc], sib_recv.at[0])
    for k in range(CHUNKS):
        wait_for(base.at[oh, oc, pl.ds(k * step, step)], sib_recv.at[1 + k])

    def multiply(kind, left, right, hc):
        @pl.loop(0, 4)
        def _(k):
            hr, cr = k // 2, k % 2
            cross[kind, hc, hr, pl.ds(pl.multiple_of(cr * cols, cols), cols), :] = lax.dot_general(
                left[hr, cr], right[...], (((0,), (0,)), ((), ())), preferred_element_type=F32
            ).astype(BF16)

    def first(kind, early):
        hc = yh if early else oh
        slot = 0 if early else 1
        for hr in range(2):
            to = 2 * hr + zs[kind] // 2
            away = (x - to + 4) % 4
            copy(
                cross.at[kind, hc, hr], line_x.at[kind, slot, away],
                x_send.at[kind, slot, hr], x_recv.at[kind, slot, away],
                device_at(to, y, z, c), to != x,
            )

    def second(kind, early):
        hc = yh if early else oh
        slot = 0 if early else 1

        @pl.when(x % 2 == zs[kind] // 2)
        def _():
            value = cross[kind, hc, x // 2].astype(F32)
            for k in range(1, 4):
                wait_for(line_x.at[kind, slot, k], x_recv.at[kind, slot, k])
                value = value + line_x[kind, slot, k].astype(F32)
            sum_x[kind, slot] = value.astype(BF16)

        to = 2 * hc + zs[kind] % 2
        away = (y - to + 4) % 4
        copy(
            sum_x.at[kind, slot], line_y.at[kind, away], l_send.at[kind, slot], l_recv.at[kind, away],
            device_at(x, to, z, c), (x % 2 == zs[kind] // 2) & (to != y),
        )

    def third(kind):
        value = sum_x[kind, 0].astype(F32)
        for k in range(1, 4):
            wait_for(line_y.at[kind, k], l_recv.at[kind, k])
            value = value + line_y[kind, k].astype(F32)
        return value / total_cells

    multiply(0, base, base.at[yh, c], yh)
    first(0, True)
    multiply(0, base, base.at[oh, c], oh)
    first(0, False)

    wait_for(north.at[yh], n_recv.at[0])
    multiply(1, base, north.at[yh], yh)
    first(1, True)

    for k in range(2):
        inside = pl.ds(k * step, step)
        wait_for(south.at[oh, c, inside], m_recv.at[1 + k])
    copy(south.at[oh, c], south.at[oh, c], ms_send.at[1], ms_recv.at[1], sibling)
    wait_for(south.at[yh, oc], ms_recv.at[0])
    wait_for(south.at[oh, oc], ms_recv.at[1])
    piece_rows = pl.ds(pl.multiple_of((z // 2) * quarter, quarter), quarter)
    multiply(2, south, north.at[yh, piece_rows], yh)
    first(2, True)

    second(0, True)
    second(0, False)

    for k in range(1, 8):
        wait_for(weights.at[k - 1], w_recv.at[k - 1])
    both = weight[...]
    for k in range(7):
        both = both + weights[k]
    scale = lax.rsqrt(both[:, cols : cols + 1] / total_cells)
    root = jnp.sqrt(jnp.float32(total_cells))
    amplitude = (root * (both[:, :cols] / total_cells)) * scale
    amps[...] = amplitude
    for k in range(2):
        modes[:, k * half : (k + 1) * half] = (proj[k] * scale).astype(BF16)
    high, low = split(amplitude)

    @pl.loop(0, 6)
    def _(k):
        at = pl.ds(pl.multiple_of(k * (cells // 6), cells // 6), cells // 6)
        block = modes[:, at]
        slow = lax.dot_general(block, high, (((0,), (0,)), ((), ())), preferred_element_type=F32)
        slow = slow + lax.dot_general(block, low, (((0,), (0,)), ((), ())), preferred_element_type=F32)
        resid[at, :] = (own[at, :].astype(F32) - slow / root).astype(BF16)

    second(1, True)
    second(2, True)

    for k in range(CHUNKS):
        wait_for(north.at[oh, pl.ds(k * step, step)], n_recv.at[1 + k])
    multiply(1, base, north.at[oh], oh)
    first(1, False)
    multiply(2, south, north.at[oh, piece_rows], oh)
    first(2, False)

    @pl.when(role == 0)
    def _():
        gram[...] = third(0)

    second(1, False)
    second(2, False)

    @pl.when(role == 0)
    def _():
        value = third(1)
        mirror[...] = value.astype(BF16)
        flipped[...] = value.T.astype(BF16)

    @pl.when(role == 3)
    def _():
        value = third(2)
        mirror[...] = value.astype(BF16)
        flipped[...] = value.T.astype(BF16)

    copy(mirror, direct, d_send, d_recv, above, sends)
    to_x, to_y = turned(x, y, z + 1)
    to_z = jnp.where(role == 0, z, z + 3)
    for k in range(2):
        copy(
            flipped.at[:, pl.ds(k * cols, cols)], flip_in.at[c], t_send.at[k], t_recv.at[c],
            device_at(to_x, to_y, to_z, k), sends,
        )

    @pl.when((role == 2) | (role == 3))
    def _():
        wait_for(direct, d_recv)
        gram[...] = direct[...].astype(F32)

    @pl.when((role == 1) | (role == 2))
    def _():
        for k in range(2):
            wait_for(flip_in.at[k], t_recv.at[k])

    @pl.when(role == 1)
    def _():
        for k in range(2):
            gram[k * cols : (k + 1) * cols, :] = flip_in[k].astype(F32)

    @pl.when(role == 2)
    def _():
        for k in range(2):
            gram[k * cols : (k + 1) * cols, :] += flip_in[k].astype(F32)

    for remote, when in pending:
        if when is None:
            remote.wait_send()
        else:
            pl.when(when)(remote.wait_send)


def body(snapshots, coefficients):
    cells, cols = snapshots.shape
    snaps, rank = coefficients.shape
    half, quarter = cells // 2, cells // 4
    dma = pltpu.SemaphoreType.DMA
    rows = 2 * cols
    gram, modes, amps, resid = pl.pallas_call(
        kernel,
        out_shape=(
            jax.ShapeDtypeStruct((rows, cols), F32),
            jax.ShapeDtypeStruct((rank, cells), BF16),
            jax.ShapeDtypeStruct((rank, cols), F32),
            jax.ShapeDtypeStruct((cells, cols), BF16),
        ),
        in_specs=[pl.BlockSpec(memory_space=pl.ANY)] * 2,
        out_specs=[pl.BlockSpec(memory_space=pltpu.VMEM)] * 4,
        scratch_shapes=[
            pltpu.VMEM((cells, cols), BF16),
            pltpu.VMEM((rank, cols), BF16),
            pltpu.VMEM((2, 2, half, cols), BF16),
            pltpu.VMEM((2, half, cols), BF16),
            pltpu.VMEM((2, 2, quarter, cols), BF16),
            pltpu.VMEM((3, 2, 2, rows, cols), BF16),
            pltpu.VMEM((3, 2, 4, rows, cols), BF16),
            pltpu.VMEM((3, 2, rows, cols), BF16),
            pltpu.VMEM((3, 4, rows, cols), BF16),
            pltpu.VMEM((rows, cols), BF16),
            pltpu.VMEM((rows, cols), BF16),
            pltpu.VMEM((cols, rows), BF16),
            pltpu.VMEM((2, cols, cols), BF16),
            pltpu.VMEM((rank, cells), F32),
            pltpu.VMEM((rank, half), F32),
            pltpu.VMEM((7, 8, half), F32),
            pltpu.VMEM((2, rank, half), F32),
            pltpu.VMEM((rank, cols + 128), F32),
            pltpu.VMEM((7, rank, cols + 128), F32),
            dma((3,)),
            dma((CHUNKS,)), dma((CHUNKS,)),
            dma((1 + CHUNKS,)), dma((1 + CHUNKS,)),
            dma((1 + CHUNKS,)), dma((1 + CHUNKS,)),
            dma((3,)), dma((3,)),
            dma((2,)), dma((2,)),
            dma((3, 2, 2)), dma((3, 2, 4)),
            dma((3, 2)), dma((3, 4)),
            dma, dma,
            dma((2,)), dma((2,)),
            dma, dma,
            dma((7,)), dma((7,)),
            dma((7,)), dma((7,)),
            dma, dma,
            dma((7,)), dma((7,)),
        ],
        compiler_params=pltpu.CompilerParams(
            collective_id=0, has_side_effects=True, vmem_limit_bytes=56 << 20
        ),
    )(snapshots, coefficients.T)
    return gram, modes.T, amps.T, resid


def solution(mesh):
    return jax.shard_map(
        body,
        mesh=mesh,
        in_specs=(P("space", "tm"), P()),
        out_specs=(P("space", "tm"), P("space", None), P("tm", None), P("space", "tm")),
        check_vma=False,
    )
```

```python
import jax
import jax.numpy as jnp
from jax import lax
from jax.experimental import pallas as pl
from jax.experimental.pallas import tpu as pltpu
from jax.sharding import PartitionSpec as P

MESH = pl.DeviceIdType.MESH
F32, BF16 = jnp.float32, jnp.bfloat16
CHUNKS = 4


def device_at(x, y, z, c):
    x, y, z = x % 4, y % 4, z % 4
    return (x * 2 + y % 2, (y // 2) * 8 + z * 2 + c)


def wait_for(ref, sem):
    pltpu.make_async_copy(ref, ref, sem).wait()


def split(value):
    high = value.astype(BF16)
    return high, (value - high.astype(F32)).astype(BF16)


def kernel(
    snaps, coeffs, gram, modes, amps, resid,
    own, coef, base, north, south,
    early, early_in, early_sum, early_x, late, late_in, late_sum, late_y,
    diag, diag_in, upright, upright_in, turned, turned_in,
    part, sib_part, pieces, proj, weight, weights,
    local_sem, y_send, y_recv, sib_send, sib_recv, n_send, n_recv, m_send, m_recv, ms_send, ms_recv,
    a_send, a_recv, b_send, b_recv, h_send, h_recv, l_send, l_recv,
    e_send, e_recv, d_send, d_recv, t_send, t_recv,
    p_send, p_recv, r_send, r_recv, g_send, g_recv, f_send, f_recv, w_send, w_recv,
):
    space, tm = lax.axis_index("space"), lax.axis_index("tm")
    x, yl, yh, z, c = space // 2, space % 2, tm // 8, (tm // 2) % 4, tm % 2
    y, chip, oh, ol, oc = 2 * yh + yl, tm // 2, 1 - yh, 1 - yl, 1 - c
    xh, xl = x // 2, x % 2
    cells, cols = own.shape
    half, quarter, step = cells // 2, cells // 4, cells // 2 // CHUNKS
    total_cells = cells * 8
    rank = coef.shape[0]
    role = (2 * xl + yl - z + 4) % 4
    pending = []

    def copy(src, dst, send, recv, device, when=None):
        remote = pltpu.make_async_remote_copy(
            src_ref=src, dst_ref=dst, send_sem=send, recv_sem=recv, device_id=device, device_id_type=MESH
        )
        if when is None:
            remote.start()
        else:
            pl.when(when)(remote.start)
        pending.append((remote, when))

    def place(src, dst, send, recv, device, here):
        copy(src, dst, send, recv, device, jnp.logical_not(here))
        pl.when(here)(pltpu.make_async_copy(src, dst, recv).start)

    sibling = device_at(x, y, z, oc)
    partner = device_at(x, y + 2, z, c)
    beside = device_at(x, 2 * yh + ol, z, c)
    across = device_at(x, 2 * oh + ol, z, c)
    below, above = device_at(x, y, z + 3, c), device_at(x, y, z + 1, c)

    z1, z3 = (z + 1) % 4, (z + 3) % 4
    diag_at = (2 * xh + z // 2, 2 * yh + z % 2)
    diag_here = (xl == z // 2) & (yl == z % 2)
    upright_at = (diag_at, (2 * xh + z3 // 2, 2 * yh + z3 % 2))
    turned_at = (2 * yh + z1 // 2, 2 * xh + z1 % 2)
    turned_here = (turned_at[0] == x) & (turned_at[1] == y) & (xl == c)

    barrier = pltpu.get_barrier_semaphore()

    def greet(device, when=None):
        def do():
            pl.semaphore_signal(barrier, inc=1, device_id=device, device_id_type=MESH)

        do() if when is None else pl.when(when)(do)

    greet(sibling)
    greet(across)
    for k in range(1, 8):
        greet((space, ((chip + k) % 8) * 2 + c))
        greet(((space + k) % 8, tm))
    for i in range(2):
        for j in range(2):
            at_x, at_y = 2 * xh + i, 2 * yh + j
            greet(device_at(at_x, at_y, z, c), (role == 0) & ((xl != i) | (yl != j)))
            greet(device_at(at_x, at_y, z + 3, c), role >= 2)
            from_x, from_y = 2 * yh + c, 2 * xh + j
            here = (from_x == x) & (from_y == y) & (c == i)
            greet(device_at(from_x, from_y, z, i), (role == 1) & jnp.logical_not(here))
            greet(device_at(from_x, from_y, z + 1, i), role == 2)

    keep = pl.ds(pl.multiple_of(yh * half, half), half)
    mine = pltpu.make_async_copy(snaps.at[keep], base.at[yh, c], local_sem.at[0])
    whole = pltpu.make_async_copy(snaps, own, local_sem.at[1])
    coef_own = pltpu.make_async_copy(
        coeffs.at[:, pl.ds(pl.multiple_of(tm * cols, cols), cols)], coef, local_sem.at[2]
    )
    coef_own.start()
    whole.start()
    mine.start()
    coef_own.wait()
    whole.wait()

    @pl.loop(0, 4)
    def _(k):
        at = pl.ds(pl.multiple_of(k * (cells // 4), cells // 4), cells // 4)
        part[:, at] = lax.dot_general(
            coef[...], own[at, :], (((1,), (1,)), ((), ())), preferred_element_type=F32
        )

    pl.semaphore_wait(barrier, 21 - diag_here.astype(jnp.int32) - turned_here.astype(jnp.int32))

    for k in range(CHUNKS):
        rows = pl.ds(pl.multiple_of(oh * half + k * step, step), step)
        copy(snaps.at[rows], base.at[yh, c, pl.ds(k * step, step)], y_send.at[k], y_recv.at[k], partner)
    other_half = pl.ds(pl.multiple_of(oc * half, half), half)
    copy(part.at[:, other_half], sib_part, p_send, p_recv, sibling)
    copy(snaps.at[keep], base.at[yh, c], sib_send.at[0], sib_recv.at[0], sibling)
    copy(snaps.at[keep], north.at[yh], n_send.at[0], n_recv.at[0], below)
    piece_for = z1 // 2
    rows = pl.ds(pl.multiple_of(yh * half + piece_for * quarter, quarter), quarter)
    copy(snaps.at[rows], south.at[yh, c], m_send.at[0], m_recv.at[0], above)

    wait_for(sib_part, p_recv)
    own_half = pl.ds(pl.multiple_of(c * half, half), half)
    sib_part[...] += part[:, own_half]
    for k in range(1, 8):
        to = (chip + k) % 8
        rows = pl.ds(pl.multiple_of(to * 8, 8), 8)
        copy(sib_part.at[rows], pieces.at[k - 1], r_send.at[k - 1], r_recv.at[k - 1], (space, to * 2 + c))

    def relay(k):
        rows = pl.ds(k * step, step)
        wait_for(base.at[oh, c, rows], y_recv.at[k])
        src = base.at[oh, c, rows]
        copy(src, base.at[oh, c, rows], sib_send.at[1 + k], sib_recv.at[1 + k], sibling)
        copy(src, north.at[oh, rows], n_send.at[1 + k], n_recv.at[1 + k], below)
        inside = pl.ds((k % 2) * step, step)
        copy(
            src, south.at[oh, c, inside], m_send.at[1 + k % 2], m_recv.at[1 + k % 2], above, piece_for == k // 2
        )

    relay(0)
    relay(1)

    for k in range(7):
        wait_for(pieces.at[k], r_recv.at[k])
    rows8 = pl.ds(pl.multiple_of(chip * 8, 8), 8)
    piece = sib_part[rows8, :]
    for k in range(7):
        piece = piece + pieces[k]
    proj[c, rows8, :] = piece
    for k in range(1, 8):
        to = (chip + k) % 8
        copy(proj.at[c, rows8], proj.at[c, rows8], g_send.at[k - 1], g_recv.at[k - 1], (space, to * 2 + c))

    relay(2)
    relay(3)
    mine.wait()

    wait_for(south.at[yh, c], m_recv.at[0])
    copy(south.at[yh, c], south.at[yh, c], ms_send.at[0], ms_recv.at[0], sibling)

    wait_for(base.at[yh, oc], sib_recv.at[0])
    for k in range(CHUNKS):
        wait_for(base.at[oh, oc, pl.ds(k * step, step)], sib_recv.at[1 + k])

    def product(left, right, k):
        return lax.dot_general(
            left[k // 2, k % 2], right[...], (((0,), (0,)), ((), ())), preferred_element_type=F32
        ).astype(BF16)

    def early_one(kind, left, right):
        @pl.loop(0, 4)
        def _(k):
            value = product(left, right, k)
            early[kind, 0, k] = value[:, : cols // 2]
            early[kind, 1, k] = value[:, cols // 2 :]

        copy(early.at[kind, ol], early_in.at[kind], a_send.at[kind], a_recv.at[kind], beside)

    def early_two(kind):
        wait_for(early_in.at[kind], a_recv.at[kind])
        early_sum[kind] = (early[kind, yl].astype(F32) + early_in[kind].astype(F32)).astype(BF16)
        for k in range(1, 4):
            copy(
                early_sum.at[kind, (x + k) % 4], early_x.at[kind, k - 1],
                b_send.at[kind, k - 1], b_recv.at[kind, k - 1], device_at(x + k, y, z, c),
            )

    def late_one(kind, left, right):
        @pl.loop(0, 4)
        def _(k):
            late[kind, k] = product(left, right, k)

        for k in range(1, 4):
            copy(
                late.at[kind, (x + k) % 4], late_in.at[kind, k - 1],
                h_send.at[kind, k - 1], h_recv.at[kind, k - 1], device_at(x + k, y, z, c),
            )

    def late_two(kind):
        value = late[kind, x].astype(F32)
        for k in range(3):
            wait_for(late_in.at[kind, k], h_recv.at[kind, k])
            value = value + late_in[kind, k].astype(F32)
        late_sum[kind, 0] = value[:, : cols // 2].astype(BF16)
        late_sum[kind, 1] = value[:, cols // 2 :].astype(BF16)
        copy(late_sum.at[kind, yl], late_y.at[kind, 0], l_send.at[kind, 0], l_recv.at[kind, 0], partner)
        copy(late_sum.at[kind, ol], late_y.at[kind, 1], l_send.at[kind, 1], l_recv.at[kind, 1], across)

    def total(kind):
        value = early_sum[kind, x].astype(F32)
        for k in range(3):
            wait_for(early_x.at[kind, k], b_recv.at[kind, k])
            value = value + early_x[kind, k].astype(F32)
        for k in range(2):
            wait_for(late_y.at[kind, k], l_recv.at[kind, k])
            value = value + late_y[kind, k].astype(F32)
        return value / total_cells

    def deliver(kind):
        value = total(kind)
        k = kind - 1
        upright[k] = value.astype(BF16)
        turned[k] = value.T.astype(BF16)
        at_x, at_y = upright_at[k]
        copy(
            upright.at[k], upright_in.at[xl, yl], d_send.at[k], d_recv.at[2 * xl + yl],
            device_at(at_x, at_y, z + 1, c),
        )
        at_x, at_y = turned_at
        dst, send, recv = turned_in.at[c, yl], t_send.at[k], t_recv.at[2 * c + yl]
        if kind == 1:
            place(turned.at[k], dst, send, recv, device_at(at_x, at_y, z, xl), turned_here)
        else:
            copy(turned.at[k], dst, send, recv, device_at(at_x, at_y, z + 3, xl))

    early_one(0, base, base.at[yh, c])
    late_one(0, base, base.at[oh, c])

    for k in range(2):
        inside = pl.ds(k * step, step)
        wait_for(south.at[oh, c, inside], m_recv.at[1 + k])
    copy(south.at[oh, c], south.at[oh, c], ms_send.at[1], ms_recv.at[1], sibling)

    wait_for(north.at[yh], n_recv.at[0])
    early_one(1, base, north.at[yh])

    for k in range(1, 8):
        rows = pl.ds(pl.multiple_of(((chip - k + 8) % 8) * 8, 8), 8)
        wait_for(proj.at[c, rows], g_recv.at[k - 1])
    copy(proj.at[c], proj.at[c], f_send, f_recv, sibling)

    wait_for(south.at[yh, oc], ms_recv.at[0])
    wait_for(south.at[oh, oc], ms_recv.at[1])
    piece_rows = pl.ds(pl.multiple_of((z // 2) * quarter, quarter), quarter)
    early_one(2, south, north.at[yh, piece_rows])

    early_two(0)

    wait_for(proj.at[oc], f_recv)
    sums = jnp.zeros((rank, cols), F32)
    squares = jnp.zeros((rank, 1), F32)
    for k in range(2):
        value = proj[k]
        squares = squares + jnp.sum(value * value, axis=1, keepdims=True)
        high, low = split(value)
        block = own[k * half : (k + 1) * half, :]
        sums = sums + jnp.dot(high, block, preferred_element_type=F32)
        sums = sums + jnp.dot(low, block, preferred_element_type=F32)
    weight[:, :cols] = sums
    weight[:, cols:] = jnp.broadcast_to(squares, (rank, 128))
    for k in range(1, 8):
        copy(weight, weights.at[k - 1], w_send.at[k - 1], w_recv.at[k - 1], ((space + k) % 8, tm))

    early_two(1)
    early_two(2)
    late_two(0)

    for k in range(CHUNKS):
        wait_for(north.at[oh, pl.ds(k * step, step)], n_recv.at[1 + k])
    late_one(1, base, north.at[oh])
    late_one(2, south, north.at[oh, piece_rows])

    diag[...] = total(0)
    place(
        diag, diag_in.at[xl, yl], e_send, e_recv.at[2 * xl + yl], device_at(*diag_at, z, c), diag_here
    )

    for k in range(1, 8):
        wait_for(weights.at[k - 1], w_recv.at[k - 1])
    both = weight[...]
    for k in range(7):
        both = both + weights[k]
    scale = lax.rsqrt(both[:, cols : cols + 1] / total_cells)
    root = jnp.sqrt(jnp.float32(total_cells))
    amplitude = (root * (both[:, :cols] / total_cells)) * scale
    amps[...] = amplitude
    for k in range(2):
        modes[:, k * half : (k + 1) * half] = (proj[k] * scale).astype(BF16)
    high, low = split(amplitude)

    late_two(1)
    late_two(2)

    @pl.loop(0, 6)
    def _(k):
        at = pl.ds(pl.multiple_of(k * (cells // 6), cells // 6), cells // 6)
        block = modes[:, at]
        slow = lax.dot_general(block, high, (((0,), (0,)), ((), ())), preferred_element_type=F32)
        slow = slow + lax.dot_general(block, low, (((0,), (0,)), ((), ())), preferred_element_type=F32)
        resid[at, :] = (own[at, :].astype(F32) - slow / root).astype(BF16)

    deliver(1)
    deliver(2)

    near = cols // 2

    @pl.when(role == 0)
    def _():
        for i in range(2):
            for j in range(2):
                wait_for(diag_in.at[i, j], e_recv.at[2 * i + j])
                gram[i * cols : (i + 1) * cols, j * near : (j + 1) * near] = diag_in[i, j]

    @pl.when(role >= 2)
    def _():
        for i in range(2):
            for j in range(2):
                wait_for(upright_in.at[i, j], d_recv.at[2 * i + j])
                gram[i * cols : (i + 1) * cols, j * near : (j + 1) * near] = upright_in[i, j].astype(F32)

    @pl.when((role == 1) | (role == 2))
    def _():
        for i in range(2):
            for j in range(2):
                wait_for(turned_in.at[i, j], t_recv.at[2 * i + j])

    @pl.when(role == 1)
    def _():
        for k in range(4):
            gram[k * near : (k + 1) * near, :] = turned_in[k // 2, k % 2].astype(F32)

    @pl.when(role == 2)
    def _():
        for k in range(4):
            gram[k * near : (k + 1) * near, :] += turned_in[k // 2, k % 2].astype(F32)

    for remote, when in pending:
        if when is None:
            remote.wait_send()
        else:
            pl.when(when)(remote.wait_send)


def body(snapshots, coefficients):
    cells, cols = snapshots.shape
    snaps, rank = coefficients.shape
    half, quarter = cells // 2, cells // 4
    dma = pltpu.SemaphoreType.DMA
    rows, near = 2 * cols, cols // 2
    gram, modes, amps, resid = pl.pallas_call(
        kernel,
        out_shape=(
            jax.ShapeDtypeStruct((rows, cols), F32),
            jax.ShapeDtypeStruct((rank, cells), BF16),
            jax.ShapeDtypeStruct((rank, cols), F32),
            jax.ShapeDtypeStruct((cells, cols), BF16),
        ),
        in_specs=[pl.BlockSpec(memory_space=pl.ANY)] * 2,
        out_specs=[pl.BlockSpec(memory_space=pltpu.VMEM)] * 4,
        scratch_shapes=[
            pltpu.VMEM((cells, cols), BF16),
            pltpu.VMEM((rank, cols), BF16),
            pltpu.VMEM((2, 2, half, cols), BF16),
            pltpu.VMEM((2, half, cols), BF16),
            pltpu.VMEM((2, 2, quarter, cols), BF16),
            pltpu.VMEM((3, 2, 4, cols, near), BF16),
            pltpu.VMEM((3, 4, cols, near), BF16),
            pltpu.VMEM((3, 4, cols, near), BF16),
            pltpu.VMEM((3, 3, cols, near), BF16),
            pltpu.VMEM((3, 4, cols, cols), BF16),
            pltpu.VMEM((3, 3, cols, cols), BF16),
            pltpu.VMEM((3, 2, cols, near), BF16),
            pltpu.VMEM((3, 2, cols, near), BF16),
            pltpu.VMEM((cols, near), F32),
            pltpu.VMEM((2, 2, cols, near), F32),
            pltpu.VMEM((2, cols, near), BF16),
            pltpu.VMEM((2, 2, cols, near), BF16),
            pltpu.VMEM((2, near, cols), BF16),
            pltpu.VMEM((2, 2, near, cols), BF16),
            pltpu.VMEM((rank, cells), F32),
            pltpu.VMEM((rank, half), F32),
            pltpu.VMEM((7, 8, half), F32),
            pltpu.VMEM((2, rank, half), F32),
            pltpu.VMEM((rank, cols + 128), F32),
            pltpu.VMEM((7, rank, cols + 128), F32),
            dma((3,)),
            dma((CHUNKS,)), dma((CHUNKS,)),
            dma((1 + CHUNKS,)), dma((1 + CHUNKS,)),
            dma((1 + CHUNKS,)), dma((1 + CHUNKS,)),
            dma((3,)), dma((3,)),
            dma((2,)), dma((2,)),
            dma((3,)), dma((3,)),
            dma((3, 3)), dma((3, 3)),
            dma((3, 3)), dma((3, 3)),
            dma((3, 2)), dma((3, 2)),
            dma, dma((4,)),
            dma((2,)), dma((4,)),
            dma((2,)), dma((4,)),
            dma, dma,
            dma((7,)), dma((7,)),
            dma((7,)), dma((7,)),
            dma, dma,
            dma((7,)), dma((7,)),
        ],
        compiler_params=pltpu.CompilerParams(
            collective_id=0, has_side_effects=True, vmem_limit_bytes=56 << 20
        ),
    )(snapshots, coefficients.T)
    return gram, modes.T, amps.T, resid


def solution(mesh):
    return jax.shard_map(
        body,
        mesh=mesh,
        in_specs=(P("space", "tm"), P()),
        out_specs=(P("space", "tm"), P("space", None), P("tm", None), P("space", "tm")),
        check_vma=False,
    )
```

```python
import jax
import jax.numpy as jnp
from jax import lax
from jax.experimental import pallas as pl
from jax.experimental.pallas import tpu as pltpu
from jax.sharding import PartitionSpec as P

MESH = pl.DeviceIdType.MESH
F32, BF16 = jnp.float32, jnp.bfloat16
CHUNKS = 4


def device_at(x, y, z, c):
    x, y, z = x & 3, y & 3, z & 3
    return (x * 2 + (y & 1), (y >> 1) * 8 + z * 2 + c)


def wait_for(ref, sem):
    pltpu.make_async_copy(ref, ref, sem).wait()


def split(value):
    high = value.astype(BF16)
    return high, (value - high.astype(F32)).astype(BF16)


def kernel(
    snaps, coeffs, gram, modes, amps, resid,
    own, coef, base, north, south,
    early, early_in, early_sum, early_x, late, late_in, late_sum, late_y,
    diag, diag_in, upright, upright_in, turned, turned_in,
    up_late, up_late_in, turned_late, turned_late_in,
    part, sib_part, pieces, proj, weight, weights,
    local_sem, y_send, y_recv, sib_send, sib_recv, n_send, n_recv, m_send, m_recv, ms_send, ms_recv,
    a_send, a_recv, b_send, b_recv, h_send, h_recv, l_send, l_recv,
    e_send, e_recv, d_send, d_recv, t_send, t_recv, q_send, q_recv, v_send, v_recv,
    p_send, p_recv, r_send, r_recv, g_send, g_recv, f_send, f_recv, w_send, w_recv,
):
    space, tm = lax.axis_index("space"), lax.axis_index("tm")
    x, yl, yh, z, c = space >> 1, space & 1, tm >> 3, (tm >> 1) & 3, tm & 1
    y, chip, oh, ol, oc = 2 * yh + yl, tm >> 1, 1 - yh, 1 - yl, 1 - c
    xh, xl = x >> 1, x & 1
    cells, cols = own.shape
    half, quarter, step = cells // 2, cells // 4, cells // 2 // CHUNKS
    total_cells = cells * 8
    rank = coef.shape[0]
    role = (2 * xl + yl - z) & 3
    pending = []

    def copy(src, dst, send, recv, device, when=None):
        remote = pltpu.make_async_remote_copy(
            src_ref=src, dst_ref=dst, send_sem=send, recv_sem=recv, device_id=device, device_id_type=MESH
        )
        if when is None:
            remote.start()
        else:
            pl.when(when)(remote.start)
        pending.append((remote, when))

    def place(src, dst, send, recv, device, here):
        copy(src, dst, send, recv, device, jnp.logical_not(here))
        pl.when(here)(pltpu.make_async_copy(src, dst, recv).start)

    sibling = device_at(x, y, z, oc)
    partner = device_at(x, y + 2, z, c)
    beside = device_at(x, 2 * yh + ol, z, c)
    across = device_at(x, 2 * oh + ol, z, c)
    below, above = device_at(x, y, z + 3, c), device_at(x, y, z + 1, c)

    z1, z3 = (z + 1) & 3, (z + 3) & 3
    diag_at = (2 * xh + (z >> 1), 2 * yh + (z & 1))
    diag_here = (xl == (z >> 1)) & (yl == (z & 1))
    turned_at = (2 * yh + (z1 >> 1), 2 * xh + (z1 & 1))
    turned_here = (turned_at[0] == x) & (turned_at[1] == y) & (xl == c)

    barrier = pltpu.get_barrier_semaphore()

    def greet(device, when=None):
        def do():
            pl.semaphore_signal(barrier, inc=1, device_id=device, device_id_type=MESH)

        do() if when is None else pl.when(when)(do)

    greet(sibling)
    greet(across)
    for k in range(1, 8):
        greet((space, ((chip + k) & 7) * 2 + c))
        greet(((space + k) & 7, tm))

    keep = pl.ds(pl.multiple_of(yh * half, half), half)
    mine = pltpu.make_async_copy(snaps.at[keep], base.at[yh, c], local_sem.at[0])
    whole = pltpu.make_async_copy(snaps, own, local_sem.at[1])
    coef_own = pltpu.make_async_copy(
        coeffs.at[:, pl.ds(pl.multiple_of(tm * cols, cols), cols)], coef, local_sem.at[2]
    )
    coef_own.start()
    whole.start()
    mine.start()
    pl.semaphore_wait(barrier, 16)

    for k in range(CHUNKS):
        rows = pl.ds(pl.multiple_of(oh * half + k * step, step), step)
        copy(snaps.at[rows], base.at[yh, c, pl.ds(k * step, step)], y_send.at[k], y_recv.at[k], partner)
    copy(snaps.at[keep], base.at[yh, c], sib_send.at[0], sib_recv.at[0], sibling)
    copy(snaps.at[keep], north.at[yh], n_send.at[0], n_recv.at[0], below)
    piece_for = z1 >> 1
    rows = pl.ds(pl.multiple_of(yh * half + piece_for * quarter, quarter), quarter)
    copy(snaps.at[rows], south.at[yh, c], m_send.at[0], m_recv.at[0], above)

    coef_own.wait()
    whole.wait()
    part[...] = lax.dot_general(coef[...], own[...], (((1,), (1,)), ((), ())), preferred_element_type=F32)
    other_half = pl.ds(pl.multiple_of(oc * half, half), half)
    copy(part.at[:, other_half], sib_part, p_send, p_recv, sibling)
    wait_for(sib_part, p_recv)
    own_half = pl.ds(pl.multiple_of(c * half, half), half)
    sib_part[...] += part[:, own_half]
    for k in range(1, 8):
        to = (chip + k) & 7
        rows = pl.ds(pl.multiple_of(to * 8, 8), 8)
        copy(sib_part.at[rows], pieces.at[k - 1], r_send.at[k - 1], r_recv.at[k - 1], (space, to * 2 + c))

    def relay(k):
        rows = pl.ds(k * step, step)
        wait_for(base.at[oh, c, rows], y_recv.at[k])
        src = base.at[oh, c, rows]
        copy(src, base.at[oh, c, rows], sib_send.at[1 + k], sib_recv.at[1 + k], sibling)
        copy(src, north.at[oh, rows], n_send.at[1 + k], n_recv.at[1 + k], below)
        inside = pl.ds((k % 2) * step, step)
        copy(
            src, south.at[oh, c, inside], m_send.at[1 + k % 2], m_recv.at[1 + k % 2], above, piece_for == k // 2
        )

    relay(0)
    relay(1)
    relay(2)
    relay(3)

    for k in range(7):
        wait_for(pieces.at[k], r_recv.at[k])
    rows8 = pl.ds(pl.multiple_of(chip * 8, 8), 8)
    piece = sib_part[rows8, :]
    for k in range(7):
        piece = piece + pieces[k]
    proj[c, rows8, :] = piece
    for k in range(1, 8):
        to = (chip + k) & 7
        copy(proj.at[c, rows8], proj.at[c, rows8], g_send.at[k - 1], g_recv.at[k - 1], (space, to * 2 + c))

    mine.wait()

    wait_for(south.at[yh, c], m_recv.at[0])
    copy(south.at[yh, c], south.at[yh, c], ms_send.at[0], ms_recv.at[0], sibling)

    wait_for(base.at[yh, oc], sib_recv.at[0])
    for k in range(CHUNKS):
        wait_for(base.at[oh, oc, pl.ds(k * step, step)], sib_recv.at[1 + k])

    def product(left, right, k):
        return lax.dot_general(
            left[k // 2, k % 2], right[...], (((0,), (0,)), ((), ())), preferred_element_type=F32
        ).astype(BF16)

    def early_one(kind, left, right):
        @pl.loop(0, 4)
        def _(k):
            value = product(left, right, k)
            early[kind, 0, k] = value[:, : cols // 2]
            early[kind, 1, k] = value[:, cols // 2 :]

        copy(early.at[kind, ol], early_in.at[kind], a_send.at[kind], a_recv.at[kind], beside)

    def early_two(kind):
        wait_for(early_in.at[kind], a_recv.at[kind])
        early_sum[kind] = (early[kind, yl].astype(F32) + early_in[kind].astype(F32)).astype(BF16)
        for k in range(1, 4):
            copy(
                early_sum.at[kind, (x + k) & 3], early_x.at[kind, k - 1],
                b_send.at[kind, k - 1], b_recv.at[kind, k - 1], device_at(x + k, y, z, c),
            )

    def late_one(kind, left, right):
        @pl.loop(0, 4)
        def _(k):
            late[kind, k] = product(left, right, k)

        for k in range(1, 4):
            copy(
                late.at[kind, (x + k) & 3], late_in.at[kind, k - 1],
                h_send.at[kind, k - 1], h_recv.at[kind, k - 1], device_at(x + k, y, z, c),
            )

    def late_total(kind):
        value = late[kind, x].astype(F32)
        for k in range(3):
            wait_for(late_in.at[kind, k], h_recv.at[kind, k])
            value = value + late_in[kind, k].astype(F32)
        return value

    def early_total(kind):
        value = early_sum[kind, x].astype(F32)
        for k in range(3):
            wait_for(early_x.at[kind, k], b_recv.at[kind, k])
            value = value + early_x[kind, k].astype(F32)
        return value

    def deliver(kind, value, at_yh, up, up_in, up_send, up_recv, over, over_in, over_send, over_recv):
        k = kind - 1
        up[k] = value.astype(BF16)
        over[k] = value.T.astype(BF16)
        row_at = z if kind == 1 else z3
        copy(
            up.at[k], up_in.at[xl, yl], up_send.at[k], up_recv.at[2 * xl + yl],
            device_at(2 * xh + (row_at >> 1), 2 * at_yh + (row_at & 1), z + 1, c),
        )
        device = device_at(2 * at_yh + (z1 >> 1), 2 * xh + (z1 & 1), z if kind == 1 else z3, xl)
        dst, recv = over_in.at[c, yl], over_recv.at[2 * c + yl]
        if kind == 1 and at_yh is yh:
            place(over.at[k], dst, over_send.at[k], recv, device, turned_here)
        else:
            copy(over.at[k], dst, over_send.at[k], recv, device)

    def deliver_early(kind):
        value = early_total(kind) / total_cells
        deliver(
            kind, value, yh, upright, upright_in, d_send, d_recv, turned, turned_in, t_send, t_recv
        )

    def deliver_late(kind):
        value = late_total(kind) / total_cells
        deliver(
            kind, value, oh, up_late, up_late_in, q_send, q_recv, turned_late, turned_late_in, v_send, v_recv
        )

    early_one(0, base, base.at[yh, c])
    late_one(0, base, base.at[oh, c])

    for k in range(2):
        inside = pl.ds(k * step, step)
        wait_for(south.at[oh, c, inside], m_recv.at[1 + k])
    copy(south.at[oh, c], south.at[oh, c], ms_send.at[1], ms_recv.at[1], sibling)

    wait_for(north.at[yh], n_recv.at[0])
    early_one(1, base, north.at[yh])

    wait_for(south.at[yh, oc], ms_recv.at[0])
    wait_for(south.at[oh, oc], ms_recv.at[1])
    piece_rows = pl.ds(pl.multiple_of((z >> 1) * quarter, quarter), quarter)
    early_one(2, south, north.at[yh, piece_rows])

    early_two(0)

    for k in range(1, 8):
        rows = pl.ds(pl.multiple_of(((chip - k) & 7) * 8, 8), 8)
        wait_for(proj.at[c, rows], g_recv.at[k - 1])
    copy(proj.at[c], proj.at[c], f_send, f_recv, sibling)

    early_two(1)
    early_two(2)

    value = late_total(0)
    late_sum[0] = value[:, : cols // 2].astype(BF16)
    late_sum[1] = value[:, cols // 2 :].astype(BF16)
    copy(late_sum.at[yl], late_y.at[0], l_send.at[0], l_recv.at[0], partner)
    copy(late_sum.at[ol], late_y.at[1], l_send.at[1], l_recv.at[1], across)

    wait_for(proj.at[oc], f_recv)
    sums = jnp.zeros((2 * rank, cols), F32)
    squares = jnp.zeros((rank, 1), F32)
    for k in range(2):
        value = proj[k]
        squares = squares + jnp.sum(value * value, axis=1, keepdims=True)
        sums = sums + jnp.dot(
            jnp.concatenate(split(value), axis=0), own[k * half : (k + 1) * half, :], preferred_element_type=F32
        )
    weight[:, :cols] = sums[:rank] + sums[rank:]
    weight[:, cols:] = jnp.broadcast_to(squares, (rank, 128))
    for k in range(1, 8):
        copy(weight, weights.at[k - 1], w_send.at[k - 1], w_recv.at[k - 1], ((space + k) & 7, tm))

    for k in range(CHUNKS):
        wait_for(north.at[oh, pl.ds(k * step, step)], n_recv.at[1 + k])
    late_one(1, base, north.at[oh])
    late_one(2, south, north.at[oh, piece_rows])

    for k in range(1, 8):
        wait_for(weights.at[k - 1], w_recv.at[k - 1])

    value = early_total(0)
    for k in range(2):
        wait_for(late_y.at[k], l_recv.at[k])
        value = value + late_y[k].astype(F32)
    diag[...] = value / total_cells
    place(
        diag, diag_in.at[xl, yl], e_send, e_recv.at[2 * xl + yl], device_at(*diag_at, z, c), diag_here
    )
    deliver_early(1)
    deliver_early(2)

    both = weight[...]
    for k in range(7):
        both = both + weights[k]
    scale = lax.rsqrt(both[:, cols : cols + 1] / total_cells)
    root = jnp.sqrt(jnp.float32(total_cells))
    amplitude = (root * (both[:, :cols] / total_cells)) * scale
    amps[...] = amplitude
    high, low = split(amplitude)

    deliver_late(1)
    deliver_late(2)

    for k in range(2):
        modes[:, k * half : (k + 1) * half] = (proj[k] * scale).astype(BF16)

    @pl.loop(0, 6)
    def _(k):
        at = pl.ds(pl.multiple_of(k * (cells // 6), cells // 6), cells // 6)
        block = modes[:, at]
        slow = lax.dot_general(block, high, (((0,), (0,)), ((), ())), preferred_element_type=F32)
        slow = slow + lax.dot_general(block, low, (((0,), (0,)), ((), ())), preferred_element_type=F32)
        resid[at, :] = (own[at, :].astype(F32) - slow / root).astype(BF16)

    near = cols // 2

    @pl.when(role == 0)
    def _():
        for i in range(2):
            for j in range(2):
                wait_for(diag_in.at[i, j], e_recv.at[2 * i + j])
                gram[i * cols : (i + 1) * cols, j * near : (j + 1) * near] = diag_in[i, j]

    def block_of(first, first_recv, last, last_recv, i, axis):
        for j in range(2):
            wait_for(first.at[i, j], first_recv.at[2 * i + j])
            wait_for(last.at[i, j], last_recv.at[2 * i + j])
        value = last[i, 0].astype(F32) + last[i, 1].astype(F32)
        return value + jnp.concatenate([first[i, 0], first[i, 1]], axis=axis).astype(F32)

    def upright_block(i):
        return block_of(upright_in, d_recv, up_late_in, q_recv, i, 1)

    def turned_block(i):
        return block_of(turned_in, t_recv, turned_late_in, v_recv, i, 0)

    @pl.when(role == 1)
    def _():
        for i in range(2):
            gram[i * cols : (i + 1) * cols, :] = turned_block(i)

    @pl.when(role == 3)
    def _():
        for i in range(2):
            gram[i * cols : (i + 1) * cols, :] = upright_block(i)

    @pl.when(role == 2)
    def _():
        for i in range(2):
            gram[i * cols : (i + 1) * cols, :] = upright_block(i) + turned_block(i)

    for remote, when in pending:
        if when is None:
            remote.wait_send()
        else:
            pl.when(when)(remote.wait_send)


def hand_over(*refs):
    sources, targets, held, sems = refs[:4], refs[4:8], refs[8:12], refs[12]
    inward = [pltpu.make_async_copy(sources[k], held[k], sems.at[0, k]) for k in range(4)]
    outward = [pltpu.make_async_copy(held[k], targets[k], sems.at[1, k]) for k in range(4)]
    for one in inward:
        one.start()
    for first, then in zip(inward, outward):
        first.wait()
        then.start()
    for one in outward:
        one.wait()


def body(snapshots, coefficients):
    cells, cols = snapshots.shape
    snaps, rank = coefficients.shape
    half, quarter = cells // 2, cells // 4
    dma = pltpu.SemaphoreType.DMA
    rows, near = 2 * cols, cols // 2
    results = pl.pallas_call(
        kernel,
        out_shape=(
            jax.ShapeDtypeStruct((rows, cols), F32),
            jax.ShapeDtypeStruct((rank, cells), BF16),
            jax.ShapeDtypeStruct((rank, cols), F32),
            jax.ShapeDtypeStruct((cells, cols), BF16),
        ),
        in_specs=[pl.BlockSpec(memory_space=pl.ANY)] * 2,
        out_specs=[pl.BlockSpec(memory_space=pltpu.VMEM)] * 4,
        scratch_shapes=[
            pltpu.VMEM((cells, cols), BF16),
            pltpu.VMEM((rank, cols), BF16),
            pltpu.VMEM((2, 2, half, cols), BF16),
            pltpu.VMEM((2, half, cols), BF16),
            pltpu.VMEM((2, 2, quarter, cols), BF16),
            pltpu.VMEM((3, 2, 4, cols, near), BF16),
            pltpu.VMEM((3, 4, cols, near), BF16),
            pltpu.VMEM((3, 4, cols, near), BF16),
            pltpu.VMEM((3, 3, cols, near), BF16),
            pltpu.VMEM((3, 4, cols, cols), BF16),
            pltpu.VMEM((3, 3, cols, cols), BF16),
            pltpu.VMEM((2, cols, near), BF16),
            pltpu.VMEM((2, cols, near), BF16),
            pltpu.VMEM((cols, near), F32),
            pltpu.VMEM((2, 2, cols, near), F32),
            pltpu.VMEM((2, cols, near), BF16),
            pltpu.VMEM((2, 2, cols, near), BF16),
            pltpu.VMEM((2, near, cols), BF16),
            pltpu.VMEM((2, 2, near, cols), BF16),
            pltpu.VMEM((2, cols, cols), BF16),
            pltpu.VMEM((2, 2, cols, cols), BF16),
            pltpu.VMEM((2, cols, cols), BF16),
            pltpu.VMEM((2, 2, cols, cols), BF16),
            pltpu.VMEM((rank, cells), F32),
            pltpu.VMEM((rank, half), F32),
            pltpu.VMEM((7, 8, half), F32),
            pltpu.VMEM((2, rank, half), F32),
            pltpu.VMEM((rank, cols + 128), F32),
            pltpu.VMEM((7, rank, cols + 128), F32),
            dma((3,)),
            dma((CHUNKS,)), dma((CHUNKS,)),
            dma((1 + CHUNKS,)), dma((1 + CHUNKS,)),
            dma((1 + CHUNKS,)), dma((1 + CHUNKS,)),
            dma((3,)), dma((3,)),
            dma((2,)), dma((2,)),
            dma((3,)), dma((3,)),
            dma((3, 3)), dma((3, 3)),
            dma((3, 3)), dma((3, 3)),
            dma((2,)), dma((2,)),
            dma, dma((4,)),
            dma((2,)), dma((4,)),
            dma((2,)), dma((4,)),
            dma((2,)), dma((4,)),
            dma((2,)), dma((4,)),
            dma, dma,
            dma((7,)), dma((7,)),
            dma((7,)), dma((7,)),
            dma, dma,
            dma((7,)), dma((7,)),
        ],
        compiler_params=pltpu.CompilerParams(
            collective_id=0, has_side_effects=True, vmem_limit_bytes=56 << 20
        ),
    )(snapshots, coefficients.T)
    gram, modes, amps, resid = pl.pallas_call(
        hand_over,
        out_shape=tuple(jax.ShapeDtypeStruct(r.shape, r.dtype) for r in results),
        in_specs=[pl.BlockSpec(memory_space=pl.ANY)] * 4,
        out_specs=[pl.BlockSpec(memory_space=pl.ANY)] * 4,
        scratch_shapes=[*(pltpu.VMEM(r.shape, r.dtype) for r in results), dma((2, 4))],
    )(*results)
    return gram, modes.T, amps.T, resid


def solution(mesh):
    return jax.shard_map(
        body,
        mesh=mesh,
        in_specs=(P("space", "tm"), P()),
        out_specs=(P("space", "tm"), P("space", None), P("tm", None), P("space", "tm")),
        check_vma=False,
    )
```

```python
import jax
import jax.numpy as jnp
from jax import lax
from jax.experimental import pallas as pl
from jax.experimental.pallas import tpu as pltpu
from jax.sharding import PartitionSpec as P

MESH = pl.DeviceIdType.MESH
F32, BF16 = jnp.float32, jnp.bfloat16
CHUNKS = 4


def device_at(x, y, z, c):
    x, y, z = x & 3, y & 3, z & 3
    return (x * 2 + (y & 1), (y >> 1) * 8 + z * 2 + c)


def wait_for(ref, sem):
    pltpu.make_async_copy(ref, ref, sem).wait()


def split(value):
    high = value.astype(BF16)
    return high, (value - high.astype(F32)).astype(BF16)


def kernel(
    snaps, coeffs, gram, modes, amps, resid,
    own, coef, base, north, south,
    early, early_in, early_sum, early_x, late, late_in, late_sum, late_y,
    diag, diag_in, upright, upright_in, turned, turned_in, passing,
    part, sib_part, pieces, proj, weight, weights, weight_sum,
    local_sem, y_send, y_recv, sib_send, sib_recv, n_send, n_recv, m_send, m_recv, ms_send, ms_recv,
    a_send, a_recv, b_send, b_recv, h_send, h_recv, l_send, l_recv,
    e_send, e_recv, d_send, d_recv, t_send, t_recv, u_send, u_recv,
    p_send, p_recv, r_send, r_recv, g_send, g_recv, f_send, f_recv, w_send, w_recv,
):
    space, tm = lax.axis_index("space"), lax.axis_index("tm")
    x, yl, yh, z, c = space >> 1, space & 1, tm >> 3, (tm >> 1) & 3, tm & 1
    y, chip, oh, ol, oc = 2 * yh + yl, tm >> 1, 1 - yh, 1 - yl, 1 - c
    xh, xl = x >> 1, x & 1
    cells, cols = own.shape
    half, quarter, near = cells // 2, cells // 4, cols // 2
    total_cells = cells * 8
    rank = coef.shape[0]
    role = (2 * xl + yl - z) & 3
    pending = []

    def copy(src, dst, send, recv, device, when=None):
        remote = pltpu.make_async_remote_copy(
            src_ref=src, dst_ref=dst, send_sem=send, recv_sem=recv, device_id=device, device_id_type=MESH
        )
        if when is None:
            remote.start()
        else:
            pl.when(when)(remote.start)
        pending.append((remote, when))

    def place(src, dst, send, recv, device, here, when=True):
        copy(src, dst, send, recv, device, jnp.logical_not(here) & when)
        pl.when(here & when)(pltpu.make_async_copy(src, dst, recv).start)

    sibling = device_at(x, y, z, oc)
    partner = device_at(x, y + 2, z, c)
    beside = device_at(x, 2 * yh + ol, z, c)
    across = device_at(x, 2 * oh + ol, z, c)
    below, above = device_at(x, y, z + 3, c), device_at(x, y, z + 1, c)

    z1, z3 = (z + 1) & 3, (z + 3) & 3
    diag_at = (2 * xh + (z >> 1), 2 * yh + (z & 1))
    diag_here = (xl == (z >> 1)) & (yl == (z & 1))
    turned_at = (2 * yh + (z1 >> 1), 2 * xh + (z1 & 1))
    turned_here = (turned_at[0] == x) & (turned_at[1] == y) & (xl == c)

    barrier = pltpu.get_barrier_semaphore()

    def greet(device, when=None):
        def do():
            pl.semaphore_signal(barrier, inc=1, device_id=device, device_id_type=MESH)

        do() if when is None else pl.when(when)(do)

    greet(sibling)
    greet(across)
    for k in range(1, 8):
        greet((space, ((chip + k) & 7) * 2 + c))
        greet(((space + k) & 7, tm))

    keep = pl.ds(pl.multiple_of(yh * half, half), half)
    mine = pltpu.make_async_copy(snaps.at[keep], base.at[yh, c], local_sem.at[0])
    whole = pltpu.make_async_copy(snaps, own, local_sem.at[1])
    coef_own = pltpu.make_async_copy(
        coeffs.at[:, pl.ds(pl.multiple_of(tm * cols, cols), cols)], coef, local_sem.at[2]
    )
    coef_own.start()
    whole.start()
    mine.start()
    pl.semaphore_wait(barrier, 16)

    for k in range(CHUNKS):
        rows = pl.ds(pl.multiple_of(oh * half + (k & 1) * quarter, quarter), quarter)
        columns = pl.ds((k >> 1) * near, near)
        copy(
            snaps.at[rows, columns], base.at[yh, c, pl.ds((k & 1) * quarter, quarter), columns],
            y_send.at[k], y_recv.at[k], partner,
        )
    copy(snaps.at[keep], base.at[yh, c], sib_send.at[0], sib_recv.at[0], sibling)
    copy(snaps.at[keep], north.at[yh], n_send.at[0], n_recv.at[0], below)
    piece_for = z1 >> 1
    rows = pl.ds(pl.multiple_of(yh * half + piece_for * quarter, quarter), quarter)
    copy(snaps.at[rows], south.at[yh, c], m_send.at[0], m_recv.at[0], above)

    coef_own.wait()
    whole.wait()
    part[...] = lax.dot_general(coef[...], own[...], (((1,), (1,)), ((), ())), preferred_element_type=F32)
    other_half = pl.ds(pl.multiple_of(oc * half, half), half)
    copy(part.at[:, other_half], sib_part, p_send, p_recv, sibling)
    wait_for(sib_part, p_recv)
    own_half = pl.ds(pl.multiple_of(c * half, half), half)
    sib_part[...] += part[:, own_half]
    for k in range(1, 8):
        to = (chip + k) & 7
        rows = pl.ds(pl.multiple_of(to * 8, 8), 8)
        copy(sib_part.at[rows], pieces.at[k - 1], r_send.at[k - 1], r_recv.at[k - 1], (space, to * 2 + c))

    def tile(k):
        return pl.ds((k & 1) * quarter, quarter), pl.ds((k >> 1) * near, near)

    def relay(k):
        rows, columns = tile(k)
        src = base.at[oh, c, rows, columns]
        wait_for(src, y_recv.at[k])
        copy(src, src, sib_send.at[1 + k], sib_recv.at[1 + k], sibling)
        copy(src, north.at[oh, rows, columns], n_send.at[1 + k], n_recv.at[1 + k], below)
        copy(
            src, south.at[oh, c, :, columns], m_send.at[1 + (k >> 1)], m_recv.at[1 + (k >> 1)], above,
            piece_for == (k & 1),
        )

    relay(0)
    relay(1)
    relay(2)
    relay(3)

    for k in range(7):
        wait_for(pieces.at[k], r_recv.at[k])
    rows8 = pl.ds(pl.multiple_of(chip * 8, 8), 8)
    piece = sib_part[rows8, :]
    for k in range(7):
        piece = piece + pieces[k]
    proj[c, rows8, :] = piece
    for k in range(1, 8):
        to = (chip + k) & 7
        copy(proj.at[c, rows8], proj.at[c, rows8], g_send.at[k - 1], g_recv.at[k - 1], (space, to * 2 + c))

    mine.wait()

    wait_for(south.at[yh, c], m_recv.at[0])
    copy(south.at[yh, c], south.at[yh, c], ms_send.at[0], ms_recv.at[0], sibling)

    wait_for(base.at[yh, oc], sib_recv.at[0])
    for k in range(CHUNKS):
        wait_for(base.at[(oh, oc, *tile(k))], sib_recv.at[1 + k])

    def product(left, right, k):
        return lax.dot_general(
            left[k // 2, k % 2], right[...], (((0,), (0,)), ((), ())), preferred_element_type=F32
        ).astype(BF16)

    def early_one(kind, left, right):
        @pl.loop(0, 4)
        def _(k):
            value = product(left, right, k)
            early[kind, 0, k] = value[:, : cols // 2]
            early[kind, 1, k] = value[:, cols // 2 :]

        copy(early.at[kind, ol], early_in.at[kind], a_send.at[kind], a_recv.at[kind], beside)

    def early_two(kind):
        wait_for(early_in.at[kind], a_recv.at[kind])
        early_sum[kind] = (early[kind, yl].astype(F32) + early_in[kind].astype(F32)).astype(BF16)
        for k in range(1, 4):
            copy(
                early_sum.at[kind, (x + k) & 3], early_x.at[kind, k - 1],
                b_send.at[kind, k - 1], b_recv.at[kind, k - 1], device_at(x + k, y, z, c),
            )

    def send_late(kind, q):
        for k in range(1, 4):
            to = (x + k) & 3
            src, dst = late.at[kind, to], late_in.at[kind, k - 1]
            if kind:
                src, dst = src.at[q], dst.at[q]
            copy(src, dst, h_send.at[kind, k - 1, q], h_recv.at[kind, k - 1, q], device_at(x + k, y, z, c))

    def late_one(kind, left, right, q):
        @pl.loop(0, 4)
        def _(k):
            late[kind, k, q] = product(left, right, k)

        send_late(kind, q)

    def late_two(kind, q):
        value = late[kind, x, q].astype(F32)
        for k in range(3):
            if kind:
                wait_for(late_in.at[kind, k, q], h_recv.at[kind, k, q])
            value = value + late_in[kind, k, q].astype(F32)
        late_sum[kind, q] = value.astype(BF16)
        copy(
            late_sum.at[kind, q], late_y.at[kind, yl ^ q], l_send.at[kind, q], l_recv.at[kind, yl ^ q],
            device_at(x, 2 * oh + q, z, c),
        )

    def total(kind):
        value = early_sum[kind, x].astype(F32)
        for k in range(3):
            wait_for(early_x.at[kind, k], b_recv.at[kind, k])
            value = value + early_x[kind, k].astype(F32)
        for k in range(2):
            wait_for(late_y.at[kind, k], l_recv.at[kind, k])
            value = value + late_y[kind, k].astype(F32)
        return value / total_cells

    def deliver(when):
        @pl.when(when)
        def _():
            for k in range(2):
                value = total(k + 1)
                upright[k] = value.astype(BF16)
                turned[k] = value.T.astype(BF16)

        for k in range(2):
            dst, send, recv = turned_in.at[c, yl], t_send.at[k], t_recv.at[2 * c + yl]
            if k == 0:
                place(turned.at[k], dst, send, recv, device_at(*turned_at, z, xl), turned_here, when)
            else:
                copy(turned.at[k], passing, send, u_recv, below, when)
            row_at = z3 if k else z
            copy(
                upright.at[k], upright_in.at[xl, yl], d_send.at[k], d_recv.at[2 * xl + yl],
                device_at(2 * xh + (row_at >> 1), 2 * yh + (row_at & 1), z + 1, c), when,
            )

    def pass_on(when):
        @pl.when(when)
        def _():
            wait_for(passing, u_recv)

        two = z ^ 2
        at_x, at_y = 2 * yh + (two >> 1), 2 * xh + (two & 1)
        here = (at_x == x) & (at_y == y) & (xl == c)
        place(
            passing, turned_in.at[c, yl], u_send, t_recv.at[2 * c + yl], device_at(at_x, at_y, z, xl), here, when
        )

    early_one(0, base, base.at[yh, c])

    @pl.loop(0, 4)
    def _(k):
        value = product(base, base.at[oh, c], k)
        late[0, k, 0] = value[:, :near]
        late[0, k, 1] = value[:, near:]

    send_late(0, 0)

    for k in range(2):
        wait_for(south.at[oh, c, :, pl.ds(k * near, near)], m_recv.at[1 + k])
    copy(south.at[oh, c], south.at[oh, c], ms_send.at[1], ms_recv.at[1], sibling)

    wait_for(north.at[yh], n_recv.at[0])
    early_one(1, base, north.at[yh])

    wait_for(south.at[yh, oc], ms_recv.at[0])
    wait_for(south.at[oh, oc], ms_recv.at[1])
    piece_rows = pl.ds(pl.multiple_of((z >> 1) * quarter, quarter), quarter)
    early_one(2, south, north.at[yh, piece_rows])

    early_two(0)

    for k in range(1, 8):
        rows = pl.ds(pl.multiple_of(((chip - k) & 7) * 8, 8), 8)
        wait_for(proj.at[c, rows], g_recv.at[k - 1])
    copy(proj.at[c], proj.at[c], f_send, f_recv, sibling)

    early_two(1)
    early_two(2)

    for k in range(3):
        wait_for(late_in.at[0, k], h_recv.at[0, k, 0])
    late_two(0, 0)
    late_two(0, 1)

    wait_for(proj.at[oc], f_recv)
    sums = jnp.zeros((2 * rank, cols), F32)
    squares = jnp.zeros((rank, 1), F32)
    for k in range(2):
        value = proj[k]
        squares = squares + jnp.sum(value * value, axis=1, keepdims=True)
        sums = sums + jnp.dot(
            jnp.concatenate(split(value), axis=0), own[k * half : (k + 1) * half, :], preferred_element_type=F32
        )
    weight[:, :cols] = sums[:rank] + sums[rank:]
    weight[:, cols:] = jnp.broadcast_to(squares, (rank, 128))
    for k in range(1, 4):
        copy(weight, weights.at[k - 1], w_send.at[k - 1], w_recv.at[k - 1], device_at(x + k, y, z, c))

    for q in range(2):
        columns = pl.ds(q * near, near)
        for k in range(2):
            wait_for(north.at[(oh, *tile(2 * q + k))], n_recv.at[1 + 2 * q + k])
        late_one(1, base, north.at[oh, :, columns], q)
        late_one(2, south, north.at[oh, piece_rows, columns], q)
        if q == 0:
            for k in range(3):
                wait_for(weights.at[k], w_recv.at[k])
            weight_sum[...] = (weight[...] + weights[0]) + (weights[1] + weights[2])
            copy(weight_sum, weights.at[3], w_send.at[3], w_recv.at[3], beside)
            late_two(1, 0)
            late_two(2, 0)

    wait_for(weights.at[3], w_recv.at[3])
    diag[...] = total(0)
    place(
        diag, diag_in.at[xl, yl], e_send, e_recv.at[2 * xl + yl], device_at(*diag_at, z, c), diag_here
    )

    deliver(yl == 0)
    late_two(1, 1)
    late_two(2, 1)
    pass_on(yl == 0)
    both = weight_sum[...] + weights[3]
    scale = lax.rsqrt(both[:, cols : cols + 1] / total_cells)
    root = jnp.sqrt(jnp.float32(total_cells))
    amplitude = (root * (both[:, :cols] / total_cells)) * scale
    amps[...] = amplitude
    high, low = split(amplitude)

    for k in range(2):
        modes[:, k * half : (k + 1) * half] = (proj[k] * scale).astype(BF16)

    deliver(yl == 1)

    @pl.loop(0, 6)
    def _(k):
        at = pl.ds(pl.multiple_of(k * (cells // 6), cells // 6), cells // 6)
        block = modes[:, at]
        slow = lax.dot_general(block, high, (((0,), (0,)), ((), ())), preferred_element_type=F32)
        slow = slow + lax.dot_general(block, low, (((0,), (0,)), ((), ())), preferred_element_type=F32)
        resid[at, :] = (own[at, :].astype(F32) - slow / root).astype(BF16)

    pass_on(yl == 1)

    @pl.when(role == 0)
    def _():
        for i in range(2):
            for j in range(2):
                wait_for(diag_in.at[i, j], e_recv.at[2 * i + j])
                gram[i * cols : (i + 1) * cols, j * near : (j + 1) * near] = diag_in[i, j]

    def block_of(tiles, recv, i, axis):
        for j in range(2):
            wait_for(tiles.at[i, j], recv.at[2 * i + j])
        return jnp.concatenate([tiles[i, 0], tiles[i, 1]], axis=axis).astype(F32)

    def upright_block(i):
        return block_of(upright_in, d_recv, i, 1)

    def turned_block(i):
        return block_of(turned_in, t_recv, i, 0)

    @pl.when(role == 1)
    def _():
        for i in range(2):
            gram[i * cols : (i + 1) * cols, :] = turned_block(i)

    @pl.when(role == 3)
    def _():
        for i in range(2):
            gram[i * cols : (i + 1) * cols, :] = upright_block(i)

    @pl.when(role == 2)
    def _():
        for i in range(2):
            gram[i * cols : (i + 1) * cols, :] = upright_block(i) + turned_block(i)

    for remote, when in pending:
        if when is None:
            remote.wait_send()
        else:
            pl.when(when)(remote.wait_send)


def hand_over(*refs):
    sources, targets, held, sems = refs[:4], refs[4:8], refs[8:12], refs[12]
    inward = [pltpu.make_async_copy(sources[k], held[k], sems.at[0, k]) for k in range(4)]
    outward = [pltpu.make_async_copy(held[k], targets[k], sems.at[1, k]) for k in range(4)]
    for one in inward:
        one.start()
    for first, then in zip(inward, outward):
        first.wait()
        then.start()
    for one in outward:
        one.wait()


def body(snapshots, coefficients):
    cells, cols = snapshots.shape
    snaps, rank = coefficients.shape
    half, quarter = cells // 2, cells // 4
    dma = pltpu.SemaphoreType.DMA
    rows, near = 2 * cols, cols // 2
    results = pl.pallas_call(
        kernel,
        out_shape=(
            jax.ShapeDtypeStruct((rows, cols), F32),
            jax.ShapeDtypeStruct((rank, cells), BF16),
            jax.ShapeDtypeStruct((rank, cols), F32),
            jax.ShapeDtypeStruct((cells, cols), BF16),
        ),
        in_specs=[pl.BlockSpec(memory_space=pl.ANY)] * 2,
        out_specs=[pl.BlockSpec(memory_space=pltpu.VMEM)] * 4,
        scratch_shapes=[
            pltpu.VMEM((cells, cols), BF16),
            pltpu.VMEM((rank, cols), BF16),
            pltpu.VMEM((2, 2, half, cols), BF16),
            pltpu.VMEM((2, half, cols), BF16),
            pltpu.VMEM((2, 2, quarter, cols), BF16),
            pltpu.VMEM((3, 2, 4, cols, near), BF16),
            pltpu.VMEM((3, 4, cols, near), BF16),
            pltpu.VMEM((3, 4, cols, near), BF16),
            pltpu.VMEM((3, 3, cols, near), BF16),
            pltpu.VMEM((3, 4, 2, cols, near), BF16),
            pltpu.VMEM((3, 3, 2, cols, near), BF16),
            pltpu.VMEM((3, 2, cols, near), BF16),
            pltpu.VMEM((3, 2, cols, near), BF16),
            pltpu.VMEM((cols, near), F32),
            pltpu.VMEM((2, 2, cols, near), F32),
            pltpu.VMEM((2, cols, near), BF16),
            pltpu.VMEM((2, 2, cols, near), BF16),
            pltpu.VMEM((2, near, cols), BF16),
            pltpu.VMEM((2, 2, near, cols), BF16),
            pltpu.VMEM((near, cols), BF16),
            pltpu.VMEM((rank, cells), F32),
            pltpu.VMEM((rank, half), F32),
            pltpu.VMEM((7, 8, half), F32),
            pltpu.VMEM((2, rank, half), F32),
            pltpu.VMEM((rank, cols + 128), F32),
            pltpu.VMEM((4, rank, cols + 128), F32),
            pltpu.VMEM((rank, cols + 128), F32),
            dma((3,)),
            dma((CHUNKS,)), dma((CHUNKS,)),
            dma((1 + CHUNKS,)), dma((1 + CHUNKS,)),
            dma((1 + CHUNKS,)), dma((1 + CHUNKS,)),
            dma((3,)), dma((3,)),
            dma((2,)), dma((2,)),
            dma((3,)), dma((3,)),
            dma((3, 3)), dma((3, 3)),
            dma((3, 3, 2)), dma((3, 3, 2)),
            dma((3, 2)), dma((3, 2)),
            dma, dma((4,)),
            dma((2,)), dma((4,)),
            dma((2,)), dma((4,)),
            dma, dma,
            dma, dma,
            dma((7,)), dma((7,)),
            dma((7,)), dma((7,)),
            dma, dma,
            dma((4,)), dma((4,)),
        ],
        compiler_params=pltpu.CompilerParams(
            collective_id=0, has_side_effects=True, vmem_limit_bytes=56 << 20
        ),
    )(snapshots, coefficients.T)
    gram, modes, amps, resid = pl.pallas_call(
        hand_over,
        out_shape=tuple(jax.ShapeDtypeStruct(r.shape, r.dtype) for r in results),
        in_specs=[pl.BlockSpec(memory_space=pl.ANY)] * 4,
        out_specs=[pl.BlockSpec(memory_space=pl.ANY)] * 4,
        scratch_shapes=[*(pltpu.VMEM(r.shape, r.dtype) for r in results), dma((2, 4))],
    )(*results)
    return gram, modes.T, amps.T, resid


def solution(mesh):
    return jax.shard_map(
        body,
        mesh=mesh,
        in_specs=(P("space", "tm"), P()),
        out_specs=(P("space", "tm"), P("space", None), P("tm", None), P("space", "tm")),
        check_vma=False,
    )
```

```python
import jax
import jax.numpy as jnp
from jax import lax
from jax.experimental import pallas as pl
from jax.experimental.pallas import tpu as pltpu
from jax.sharding import PartitionSpec as P

MESH = pl.DeviceIdType.MESH
F32, BF16 = jnp.float32, jnp.bfloat16
CHUNKS = 4


def device_at(x, y, z, c):
    x, y, z = x & 3, y & 3, z & 3
    return (x * 2 + (y & 1), (y >> 1) * 8 + z * 2 + c)


def wait_for(ref, sem):
    pltpu.make_async_copy(ref, ref, sem).wait()


def split(value):
    high = value.astype(BF16)
    return high, (value - high.astype(F32)).astype(BF16)


def kernel(
    snaps, coeffs, gram, modes, amps, resid,
    own, coef, base, north, south,
    early, early_in, early_sum, early_x, late, late_in, late_sum, late_y,
    diag, diag_in, upright, upright_in, turned, turned_in, passing,
    part, sib_part, pieces, proj, weight, weights, weight_sum,
    local_sem, y_send, y_recv, sib_send, sib_recv, n_send, n_recv, m_send, m_recv, ms_send, ms_recv,
    a_send, a_recv, b_send, b_recv, h_send, h_recv, l_send, l_recv,
    e_send, e_recv, d_send, d_recv, t_send, t_recv, u_send, u_recv,
    p_send, p_recv, r_send, r_recv, g_send, g_recv, f_send, f_recv, w_send, w_recv,
):
    space, tm = lax.axis_index("space"), lax.axis_index("tm")
    x, yl, yh, z, c = space >> 1, space & 1, tm >> 3, (tm >> 1) & 3, tm & 1
    y, chip, oh, ol, oc = 2 * yh + yl, tm >> 1, 1 - yh, 1 - yl, 1 - c
    xh, xl = x >> 1, x & 1
    cells, cols = own.shape
    half, quarter, near = cells // 2, cells // 4, cols // 2
    total_cells = cells * 8
    rank = coef.shape[0]
    role = (2 * xl + yl - z) & 3
    pending = []

    def copy(src, dst, send, recv, device, when=None):
        remote = pltpu.make_async_remote_copy(
            src_ref=src, dst_ref=dst, send_sem=send, recv_sem=recv, device_id=device, device_id_type=MESH
        )
        if when is None:
            remote.start()
        else:
            pl.when(when)(remote.start)
        pending.append((remote, when))

    def place(src, dst, send, recv, device, here, when=True):
        copy(src, dst, send, recv, device, jnp.logical_not(here) & when)
        pl.when(here & when)(pltpu.make_async_copy(src, dst, recv).start)

    sibling = device_at(x, y, z, oc)
    partner = device_at(x, y + 2, z, c)
    beside = device_at(x, 2 * yh + ol, z, c)
    across = device_at(x, 2 * oh + ol, z, c)
    below, above = device_at(x, y, z + 3, c), device_at(x, y, z + 1, c)

    z1, z3 = (z + 1) & 3, (z + 3) & 3
    diag_at = (2 * xh + (z >> 1), 2 * yh + (z & 1))
    diag_here = (xl == (z >> 1)) & (yl == (z & 1))
    turned_at = (2 * yh + (z1 >> 1), 2 * xh + (z1 & 1))
    turned_here = (turned_at[0] == x) & (turned_at[1] == y) & (xl == c)

    barrier = pltpu.get_barrier_semaphore()

    def greet(device, when=None):
        def do():
            pl.semaphore_signal(barrier, inc=1, device_id=device, device_id_type=MESH)

        do() if when is None else pl.when(when)(do)

    for device in (sibling, beside):
        greet(device)
    for k in range(1, 8):
        greet((space, ((chip + k) & 7) * 2 + c))
    for k in range(1, 4):
        greet(device_at(x + k, y, z, c))

    keep = pl.ds(pl.multiple_of(yh * half, half), half)
    mine = pltpu.make_async_copy(snaps.at[keep], base.at[yh, c], local_sem.at[0])
    whole = pltpu.make_async_copy(snaps, own, local_sem.at[1])
    coef_own = pltpu.make_async_copy(
        coeffs.at[:, pl.ds(pl.multiple_of(tm * cols, cols), cols)], coef, local_sem.at[2]
    )
    coef_own.start()
    whole.start()
    mine.start()
    pl.semaphore_wait(barrier, 12)

    for k in range(CHUNKS):
        rows = pl.ds(pl.multiple_of(oh * half + (k & 1) * quarter, quarter), quarter)
        columns = pl.ds((k >> 1) * near, near)
        copy(
            snaps.at[rows, columns], base.at[yh, c, pl.ds((k & 1) * quarter, quarter), columns],
            y_send.at[k], y_recv.at[k], partner,
        )
    copy(snaps.at[keep], base.at[yh, c], sib_send.at[0], sib_recv.at[0], sibling)
    copy(snaps.at[keep], north.at[yh], n_send.at[0], n_recv.at[0], below)
    piece_for = z1 >> 1
    rows = pl.ds(pl.multiple_of(yh * half + piece_for * quarter, quarter), quarter)
    copy(snaps.at[rows], south.at[yh, c], m_send.at[0], m_recv.at[0], above)

    coef_own.wait()
    whole.wait()
    part[...] = lax.dot_general(coef[...], own[...], (((1,), (1,)), ((), ())), preferred_element_type=F32)
    other_half = pl.ds(pl.multiple_of(oc * half, half), half)
    copy(part.at[:, other_half], sib_part, p_send, p_recv, sibling)
    wait_for(sib_part, p_recv)
    own_half = pl.ds(pl.multiple_of(c * half, half), half)
    sib_part[...] += part[:, own_half]
    for k in range(1, 8):
        to = (chip + k) & 7
        rows = pl.ds(pl.multiple_of(to * 8, 8), 8)
        copy(sib_part.at[rows], pieces.at[k - 1], r_send.at[k - 1], r_recv.at[k - 1], (space, to * 2 + c))

    def tile(k):
        return pl.ds((k & 1) * quarter, quarter), pl.ds((k >> 1) * near, near)

    def relay(k):
        rows, columns = tile(k)
        src = base.at[oh, c, rows, columns]
        wait_for(src, y_recv.at[k])
        copy(src, src, sib_send.at[1 + k], sib_recv.at[1 + k], sibling)
        copy(src, north.at[oh, rows, columns], n_send.at[1 + k], n_recv.at[1 + k], below)
        copy(
            src, south.at[oh, c, :, columns], m_send.at[1 + (k >> 1)], m_recv.at[1 + (k >> 1)], above,
            piece_for == (k & 1),
        )

    relay(0)
    relay(1)
    relay(2)
    relay(3)

    for k in range(7):
        wait_for(pieces.at[k], r_recv.at[k])
    rows8 = pl.ds(pl.multiple_of(chip * 8, 8), 8)
    piece = sib_part[rows8, :]
    for k in range(7):
        piece = piece + pieces[k]
    proj[c, rows8, :] = piece
    for k in range(1, 8):
        to = (chip + k) & 7
        copy(proj.at[c, rows8], proj.at[c, rows8], g_send.at[k - 1], g_recv.at[k - 1], (space, to * 2 + c))

    mine.wait()

    wait_for(south.at[yh, c], m_recv.at[0])
    copy(south.at[yh, c], south.at[yh, c], ms_send.at[0], ms_recv.at[0], sibling)

    wait_for(base.at[yh, oc], sib_recv.at[0])
    for k in range(CHUNKS):
        wait_for(base.at[(oh, oc, *tile(k))], sib_recv.at[1 + k])

    def product(left, right, k):
        return lax.dot_general(
            left[k // 2, k % 2], right[...], (((0,), (0,)), ((), ())), preferred_element_type=F32
        ).astype(BF16)

    def early_one(kind, left, right):
        @pl.loop(0, 4)
        def _(k):
            value = product(left, right, k)
            early[kind, 0, k] = value[:, : cols // 2]
            early[kind, 1, k] = value[:, cols // 2 :]

        copy(early.at[kind, ol], early_in.at[kind], a_send.at[kind], a_recv.at[kind], beside)

    def early_two(kind):
        wait_for(early_in.at[kind], a_recv.at[kind])
        early_sum[kind] = (early[kind, yl].astype(F32) + early_in[kind].astype(F32)).astype(BF16)
        for k in range(1, 4):
            copy(
                early_sum.at[kind, (x + k) & 3], early_x.at[kind, k - 1],
                b_send.at[kind, k - 1], b_recv.at[kind, k - 1], device_at(x + k, y, z, c),
            )

    def send_late(kind, q):
        for k in range(1, 4):
            to = (x + k) & 3
            src, dst = late.at[kind, to], late_in.at[kind, k - 1]
            if kind:
                src, dst = src.at[q], dst.at[q]
            copy(src, dst, h_send.at[kind, k - 1, q], h_recv.at[kind, k - 1, q], device_at(x + k, y, z, c))

    def late_one(kind, left, right, q):
        @pl.loop(0, 4)
        def _(k):
            late[kind, k, q] = product(left, right, k)

        send_late(kind, q)

    def late_two(kind, q):
        value = late[kind, x, q].astype(F32)
        for k in range(3):
            if kind:
                wait_for(late_in.at[kind, k, q], h_recv.at[kind, k, q])
            value = value + late_in[kind, k, q].astype(F32)
        late_sum[kind, q] = value.astype(BF16)
        copy(
            late_sum.at[kind, q], late_y.at[kind, yl ^ q], l_send.at[kind, q], l_recv.at[kind, yl ^ q],
            device_at(x, 2 * oh + q, z, c),
        )

    def total(kind):
        value = early_sum[kind, x].astype(F32)
        for k in range(3):
            wait_for(early_x.at[kind, k], b_recv.at[kind, k])
            value = value + early_x[kind, k].astype(F32)
        for k in range(2):
            wait_for(late_y.at[kind, k], l_recv.at[kind, k])
            value = value + late_y[kind, k].astype(F32)
        return value / total_cells

    def deliver(when):
        @pl.when(when)
        def _():
            for k in range(2):
                value = total(k + 1)
                upright[k] = value.astype(BF16)
                turned[k] = value.T.astype(BF16)

        for k in range(2):
            dst, send, recv = turned_in.at[c, yl], t_send.at[k], t_recv.at[2 * c + yl]
            if k == 0:
                place(turned.at[k], dst, send, recv, device_at(*turned_at, z, xl), turned_here, when)
            else:
                copy(turned.at[k], passing, send, u_recv, below, when)
            row_at = z3 if k else z
            copy(
                upright.at[k], upright_in.at[xl, yl], d_send.at[k], d_recv.at[2 * xl + yl],
                device_at(2 * xh + (row_at >> 1), 2 * yh + (row_at & 1), z + 1, c), when,
            )

    def pass_on(when):
        @pl.when(when)
        def _():
            wait_for(passing, u_recv)

        two = z ^ 2
        at_x, at_y = 2 * yh + (two >> 1), 2 * xh + (two & 1)
        here = (at_x == x) & (at_y == y) & (xl == c)
        place(
            passing, turned_in.at[c, yl], u_send, t_recv.at[2 * c + yl], device_at(at_x, at_y, z, xl), here, when
        )

    early_one(0, base, base.at[yh, c])

    @pl.loop(0, 4)
    def _(k):
        value = product(base, base.at[oh, c], k)
        late[0, k, 0] = value[:, :near]
        late[0, k, 1] = value[:, near:]

    send_late(0, 0)

    for k in range(2):
        wait_for(south.at[oh, c, :, pl.ds(k * near, near)], m_recv.at[1 + k])
    copy(south.at[oh, c], south.at[oh, c], ms_send.at[1], ms_recv.at[1], sibling)

    wait_for(north.at[yh], n_recv.at[0])
    early_one(1, base, north.at[yh])

    wait_for(south.at[yh, oc], ms_recv.at[0])
    wait_for(south.at[oh, oc], ms_recv.at[1])
    piece_rows = pl.ds(pl.multiple_of((z >> 1) * quarter, quarter), quarter)
    early_one(2, south, north.at[yh, piece_rows])

    early_two(0)

    early_two(1)
    early_two(2)

    for k in range(3):
        wait_for(late_in.at[0, k], h_recv.at[0, k, 0])
    late_two(0, 0)
    late_two(0, 1)

    for q in range(2):
        columns = pl.ds(q * near, near)
        for k in range(2):
            wait_for(north.at[(oh, *tile(2 * q + k))], n_recv.at[1 + 2 * q + k])
        late_one(1, base, north.at[oh, :, columns], q)
        late_one(2, south, north.at[oh, piece_rows, columns], q)
        if q == 0:
            late_two(1, 0)
            late_two(2, 0)

    for k in range(1, 8):
        rows = pl.ds(pl.multiple_of(((chip - k) & 7) * 8, 8), 8)
        wait_for(proj.at[c, rows], g_recv.at[k - 1])
    copy(proj.at[c], proj.at[c], f_send, f_recv, sibling)

    diag[...] = total(0)
    place(
        diag, diag_in.at[xl, yl], e_send, e_recv.at[2 * xl + yl], device_at(*diag_at, z, c), diag_here
    )

    deliver(yl == 0)
    wait_for(proj.at[oc], f_recv)
    sums = jnp.zeros((2 * rank, cols), F32)
    squares = jnp.zeros((rank, 1), F32)
    for k in range(2):
        value = proj[k]
        squares = squares + jnp.sum(value * value, axis=1, keepdims=True)
        sums = sums + jnp.dot(
            jnp.concatenate(split(value), axis=0), own[k * half : (k + 1) * half, :], preferred_element_type=F32
        )
    weight[:, :cols] = sums[:rank] + sums[rank:]
    weight[:, cols:] = jnp.broadcast_to(squares, (rank, 128))
    for k in range(1, 4):
        copy(weight, weights.at[k - 1], w_send.at[k - 1], w_recv.at[k - 1], device_at(x + k, y, z, c))

    late_two(1, 1)
    late_two(2, 1)
    for k in range(3):
        wait_for(weights.at[k], w_recv.at[k])
    weight_sum[...] = (weight[...] + weights[0]) + (weights[1] + weights[2])
    copy(weight_sum, weights.at[3], w_send.at[3], w_recv.at[3], beside)
    pass_on(yl == 0)
    deliver(yl == 1)
    wait_for(weights.at[3], w_recv.at[3])
    both = weight_sum[...] + weights[3]
    scale = lax.rsqrt(both[:, cols : cols + 1] / total_cells)
    root = jnp.sqrt(jnp.float32(total_cells))
    amplitude = (root * (both[:, :cols] / total_cells)) * scale
    amps[...] = amplitude
    high, low = split(amplitude)

    for k in range(2):
        modes[:, k * half : (k + 1) * half] = (proj[k] * scale).astype(BF16)


    @pl.loop(0, 6)
    def _(k):
        at = pl.ds(pl.multiple_of(k * (cells // 6), cells // 6), cells // 6)
        block = modes[:, at]
        slow = lax.dot_general(block, high, (((0,), (0,)), ((), ())), preferred_element_type=F32)
        slow = slow + lax.dot_general(block, low, (((0,), (0,)), ((), ())), preferred_element_type=F32)
        resid[at, :] = (own[at, :].astype(F32) - slow / root).astype(BF16)

    pass_on(yl == 1)

    @pl.when(role == 0)
    def _():
        for i in range(2):
            for j in range(2):
                wait_for(diag_in.at[i, j], e_recv.at[2 * i + j])
                gram[i * cols : (i + 1) * cols, j * near : (j + 1) * near] = diag_in[i, j]

    def block_of(tiles, recv, i, axis):
        for j in range(2):
            wait_for(tiles.at[i, j], recv.at[2 * i + j])
        return jnp.concatenate([tiles[i, 0], tiles[i, 1]], axis=axis).astype(F32)

    def upright_block(i):
        return block_of(upright_in, d_recv, i, 1)

    def turned_block(i):
        return block_of(turned_in, t_recv, i, 0)

    @pl.when(role == 1)
    def _():
        for i in range(2):
            gram[i * cols : (i + 1) * cols, :] = turned_block(i)

    @pl.when(role == 3)
    def _():
        for i in range(2):
            gram[i * cols : (i + 1) * cols, :] = upright_block(i)

    @pl.when(role == 2)
    def _():
        for i in range(2):
            gram[i * cols : (i + 1) * cols, :] = upright_block(i) + turned_block(i)

    for remote, when in pending:
        if when is None:
            remote.wait_send()
        else:
            pl.when(when)(remote.wait_send)


def hand_over(*refs):
    sources, targets, held, sems = refs[:4], refs[4:8], refs[8:12], refs[12]
    inward = [pltpu.make_async_copy(sources[k], held[k], sems.at[0, k]) for k in range(4)]
    outward = [pltpu.make_async_copy(held[k], targets[k], sems.at[1, k]) for k in range(4)]
    for one in inward:
        one.start()
    for first, then in zip(inward, outward):
        first.wait()
        then.start()
    for one in outward:
        one.wait()


def body(snapshots, coefficients):
    cells, cols = snapshots.shape
    snaps, rank = coefficients.shape
    half, quarter = cells // 2, cells // 4
    dma = pltpu.SemaphoreType.DMA
    rows, near = 2 * cols, cols // 2
    results = pl.pallas_call(
        kernel,
        out_shape=(
            jax.ShapeDtypeStruct((rows, cols), F32),
            jax.ShapeDtypeStruct((rank, cells), BF16),
            jax.ShapeDtypeStruct((rank, cols), F32),
            jax.ShapeDtypeStruct((cells, cols), BF16),
        ),
        in_specs=[pl.BlockSpec(memory_space=pl.ANY)] * 2,
        out_specs=[pl.BlockSpec(memory_space=pltpu.VMEM)] * 4,
        scratch_shapes=[
            pltpu.VMEM((cells, cols), BF16),
            pltpu.VMEM((rank, cols), BF16),
            pltpu.VMEM((2, 2, half, cols), BF16),
            pltpu.VMEM((2, half, cols), BF16),
            pltpu.VMEM((2, 2, quarter, cols), BF16),
            pltpu.VMEM((3, 2, 4, cols, near), BF16),
            pltpu.VMEM((3, 4, cols, near), BF16),
            pltpu.VMEM((3, 4, cols, near), BF16),
            pltpu.VMEM((3, 3, cols, near), BF16),
            pltpu.VMEM((3, 4, 2, cols, near), BF16),
            pltpu.VMEM((3, 3, 2, cols, near), BF16),
            pltpu.VMEM((3, 2, cols, near), BF16),
            pltpu.VMEM((3, 2, cols, near), BF16),
            pltpu.VMEM((cols, near), F32),
            pltpu.VMEM((2, 2, cols, near), F32),
            pltpu.VMEM((2, cols, near), BF16),
            pltpu.VMEM((2, 2, cols, near), BF16),
            pltpu.VMEM((2, near, cols), BF16),
            pltpu.VMEM((2, 2, near, cols), BF16),
            pltpu.VMEM((near, cols), BF16),
            pltpu.VMEM((rank, cells), F32),
            pltpu.VMEM((rank, half), F32),
            pltpu.VMEM((7, 8, half), F32),
            pltpu.VMEM((2, rank, half), F32),
            pltpu.VMEM((rank, cols + 128), F32),
            pltpu.VMEM((4, rank, cols + 128), F32),
            pltpu.VMEM((rank, cols + 128), F32),
            dma((3,)),
            dma((CHUNKS,)), dma((CHUNKS,)),
            dma((1 + CHUNKS,)), dma((1 + CHUNKS,)),
            dma((1 + CHUNKS,)), dma((1 + CHUNKS,)),
            dma((3,)), dma((3,)),
            dma((2,)), dma((2,)),
            dma((3,)), dma((3,)),
            dma((3, 3)), dma((3, 3)),
            dma((3, 3, 2)), dma((3, 3, 2)),
            dma((3, 2)), dma((3, 2)),
            dma, dma((4,)),
            dma((2,)), dma((4,)),
            dma((2,)), dma((4,)),
            dma, dma,
            dma, dma,
            dma((7,)), dma((7,)),
            dma((7,)), dma((7,)),
            dma, dma,
            dma((4,)), dma((4,)),
        ],
        compiler_params=pltpu.CompilerParams(
            collective_id=0, has_side_effects=True, vmem_limit_bytes=56 << 20
        ),
    )(snapshots, coefficients.T)
    gram, modes, amps, resid = pl.pallas_call(
        hand_over,
        out_shape=tuple(jax.ShapeDtypeStruct(r.shape, r.dtype) for r in results),
        in_specs=[pl.BlockSpec(memory_space=pl.ANY)] * 4,
        out_specs=[pl.BlockSpec(memory_space=pl.ANY)] * 4,
        scratch_shapes=[*(pltpu.VMEM(r.shape, r.dtype) for r in results), dma((2, 4))],
    )(*results)
    return gram, modes.T, amps.T, resid


def solution(mesh):
    return jax.shard_map(
        body,
        mesh=mesh,
        in_specs=(P("space", "tm"), P()),
        out_specs=(P("space", "tm"), P("space", None), P("tm", None), P("space", "tm")),
        check_vma=False,
    )
```

```python
import jax
import jax.numpy as jnp
from jax import lax
from jax.experimental import pallas as pl
from jax.experimental.pallas import tpu as pltpu
from jax.sharding import PartitionSpec as P

MESH = pl.DeviceIdType.MESH
F32, BF16 = jnp.float32, jnp.bfloat16
CHUNKS = 4


def device_at(x, y, z, c):
    x, y, z = x & 3, y & 3, z & 3
    return (x * 2 + (y & 1), (y >> 1) * 8 + z * 2 + c)


def wait_for(ref, sem):
    pltpu.make_async_copy(ref, ref, sem).wait()


def split(value):
    high = value.astype(BF16)
    return high, (value - high.astype(F32)).astype(BF16)


def kernel(
    snaps, coeffs, gram, modes, amps, resid,
    own, coef, base, north, south,
    early, early_in, early_sum, early_x, late, late_in, late_sum, late_y,
    diag, diag_in, upright, upright_in, turned, turned_in, passing,
    part, sib_part, pieces, proj, weight, weights, weight_sum,
    local_sem, y_send, y_recv, sib_send, sib_recv, n_send, n_recv, m_send, m_recv, ms_send, ms_recv,
    a_send, a_recv, b_send, b_recv, h_send, h_recv, l_send, l_recv,
    e_send, e_recv, d_send, d_recv, t_send, t_recv, u_send, u_recv,
    p_send, p_recv, r_send, r_recv, g_send, g_recv, f_send, f_recv, w_send, w_recv,
):
    space, tm = lax.axis_index("space"), lax.axis_index("tm")
    x, yl, yh, z, c = space >> 1, space & 1, tm >> 3, (tm >> 1) & 3, tm & 1
    y, chip, oh, ol, oc = 2 * yh + yl, tm >> 1, 1 - yh, 1 - yl, 1 - c
    xh, xl = x >> 1, x & 1
    cells, cols = own.shape
    half, quarter, near = cells // 2, cells // 4, cols // 2
    total_cells = cells * 8
    rank = coef.shape[0]
    role = (2 * xl + yl - z) & 3
    pending = []

    def copy(src, dst, send, recv, device, when=None):
        remote = pltpu.make_async_remote_copy(
            src_ref=src, dst_ref=dst, send_sem=send, recv_sem=recv, device_id=device, device_id_type=MESH
        )
        if when is None:
            remote.start()
        else:
            pl.when(when)(remote.start)
        pending.append((remote, when))

    def place(src, dst, send, recv, device, here, when=True):
        copy(src, dst, send, recv, device, jnp.logical_not(here) & when)
        pl.when(here & when)(pltpu.make_async_copy(src, dst, recv).start)

    sibling = device_at(x, y, z, oc)
    partner = device_at(x, y + 2, z, c)
    beside = device_at(x, 2 * yh + ol, z, c)
    across = device_at(x, 2 * oh + ol, z, c)
    below, above = device_at(x, y, z + 3, c), device_at(x, y, z + 1, c)

    z1, z3 = (z + 1) & 3, (z + 3) & 3
    diag_at = (2 * xh + (z >> 1), 2 * yh + (z & 1))
    diag_here = (xl == (z >> 1)) & (yl == (z & 1))
    turned_at = (2 * yh + (z1 >> 1), 2 * xh + (z1 & 1))
    turned_here = (turned_at[0] == x) & (turned_at[1] == y) & (xl == c)

    barrier = pltpu.get_barrier_semaphore()

    def greet(device, when=None):
        def do():
            pl.semaphore_signal(barrier, inc=1, device_id=device, device_id_type=MESH)

        do() if when is None else pl.when(when)(do)

    for device in (sibling, beside):
        greet(device)
    for k in range(1, 8):
        greet((space, ((chip + k) & 7) * 2 + c))
    for k in range(1, 4):
        greet(device_at(x + k, y, z, c))

    keep = pl.ds(pl.multiple_of(yh * half, half), half)
    mine = pltpu.make_async_copy(snaps.at[keep], base.at[yh, c], local_sem.at[0])
    whole = pltpu.make_async_copy(snaps, own, local_sem.at[1])
    coef_own = pltpu.make_async_copy(
        coeffs.at[:, pl.ds(pl.multiple_of(tm * cols, cols), cols)], coef, local_sem.at[2]
    )
    coef_own.start()
    whole.start()
    mine.start()
    pl.semaphore_wait(barrier, 12)

    for k in range(CHUNKS):
        rows = pl.ds(pl.multiple_of(oh * half + (k & 1) * quarter, quarter), quarter)
        columns = pl.ds((k >> 1) * near, near)
        copy(
            snaps.at[rows, columns], base.at[yh, c, pl.ds((k & 1) * quarter, quarter), columns],
            y_send.at[k], y_recv.at[k], partner,
        )
    copy(snaps.at[keep], base.at[yh, c], sib_send.at[0], sib_recv.at[0], sibling)
    copy(snaps.at[keep], north.at[yh], n_send.at[0], n_recv.at[0], below)
    piece_for = z1 >> 1
    rows = pl.ds(pl.multiple_of(yh * half + piece_for * quarter, quarter), quarter)
    copy(snaps.at[rows], south.at[yh, c], m_send.at[0], m_recv.at[0], above)

    coef_own.wait()
    whole.wait()
    part[...] = lax.dot_general(coef[...], own[...], (((1,), (1,)), ((), ())), preferred_element_type=F32)
    other_half = pl.ds(pl.multiple_of(oc * half, half), half)
    copy(part.at[:, other_half], sib_part, p_send, p_recv, sibling)
    wait_for(sib_part, p_recv)
    own_half = pl.ds(pl.multiple_of(c * half, half), half)
    sib_part[...] += part[:, own_half]
    for k in range(1, 8):
        to = (chip + k) & 7
        rows = pl.ds(pl.multiple_of(to * 8, 8), 8)
        copy(sib_part.at[rows], pieces.at[k - 1], r_send.at[k - 1], r_recv.at[k - 1], (space, to * 2 + c))

    def tile(k):
        return pl.ds((k & 1) * quarter, quarter), pl.ds((k >> 1) * near, near)

    def relay(k):
        rows, columns = tile(k)
        src = base.at[oh, c, rows, columns]
        wait_for(src, y_recv.at[k])
        copy(src, src, sib_send.at[1 + k], sib_recv.at[1 + k], sibling)
        copy(src, north.at[oh, rows, columns], n_send.at[1 + k], n_recv.at[1 + k], below)
        copy(
            src, south.at[oh, c, :, columns], m_send.at[1 + (k >> 1)], m_recv.at[1 + (k >> 1)], above,
            piece_for == (k & 1),
        )

    relay(0)
    relay(1)
    relay(2)
    relay(3)

    for k in range(7):
        wait_for(pieces.at[k], r_recv.at[k])
    rows8 = pl.ds(pl.multiple_of(chip * 8, 8), 8)
    piece = sib_part[rows8, :]
    for k in range(7):
        piece = piece + pieces[k]
    proj[c, rows8, :] = piece
    for k in range(1, 8):
        to = (chip + k) & 7
        copy(proj.at[c, rows8], proj.at[c, rows8], g_send.at[k - 1], g_recv.at[k - 1], (space, to * 2 + c))

    mine.wait()

    wait_for(south.at[yh, c], m_recv.at[0])
    copy(south.at[yh, c], south.at[yh, c], ms_send.at[0], ms_recv.at[0], sibling)

    wait_for(base.at[yh, oc], sib_recv.at[0])
    for k in range(CHUNKS):
        wait_for(base.at[(oh, oc, *tile(k))], sib_recv.at[1 + k])

    def product(left, right, k):
        return lax.dot_general(
            left[k // 2, k % 2], right[...], (((0,), (0,)), ((), ())), preferred_element_type=F32
        ).astype(BF16)

    def early_one(kind, left, right):
        @pl.loop(0, 4)
        def _(k):
            value = product(left, right, k)
            early[kind, 0, k] = value[:, : cols // 2]
            early[kind, 1, k] = value[:, cols // 2 :]

        copy(early.at[kind, ol], early_in.at[kind], a_send.at[kind], a_recv.at[kind], beside)

    def early_two(kind):
        wait_for(early_in.at[kind], a_recv.at[kind])
        early_sum[kind] = (early[kind, yl].astype(F32) + early_in[kind].astype(F32)).astype(BF16)
        for k in range(1, 4):
            copy(
                early_sum.at[kind, (x + k) & 3], early_x.at[kind, k - 1],
                b_send.at[kind, k - 1], b_recv.at[kind, k - 1], device_at(x + k, y, z, c),
            )

    def send_late(kind, q):
        for k in range(1, 4):
            to = (x + k) & 3
            src, dst = late.at[kind, to], late_in.at[kind, k - 1]
            if kind:
                src, dst = src.at[q], dst.at[q]
            copy(src, dst, h_send.at[kind, k - 1, q], h_recv.at[kind, k - 1, q], device_at(x + k, y, z, c))

    def late_one(kind, left, right, q):
        @pl.loop(0, 4)
        def _(k):
            late[kind, k, q] = product(left, right, k)

        send_late(kind, q)

    def late_two(kind, q):
        value = late[kind, x, q].astype(F32)
        for k in range(3):
            if kind:
                wait_for(late_in.at[kind, k, q], h_recv.at[kind, k, q])
            value = value + late_in[kind, k, q].astype(F32)
        late_sum[kind, q] = value.astype(BF16)
        copy(
            late_sum.at[kind, q], late_y.at[kind, yl ^ q], l_send.at[kind, q], l_recv.at[kind, yl ^ q],
            device_at(x, 2 * oh + q, z, c),
        )

    def total(kind):
        value = early_sum[kind, x].astype(F32)
        for k in range(3):
            wait_for(early_x.at[kind, k], b_recv.at[kind, k])
            value = value + early_x[kind, k].astype(F32)
        for k in range(2):
            wait_for(late_y.at[kind, k], l_recv.at[kind, k])
            value = value + late_y[kind, k].astype(F32)
        return value / total_cells

    def deliver(when):
        @pl.when(when)
        def _():
            for k in range(2):
                value = total(k + 1)
                upright[k] = value.astype(BF16)
                turned[k] = value.T.astype(BF16)

        for k in range(2):
            dst, send, recv = turned_in.at[c, yl], t_send.at[k], t_recv.at[2 * c + yl]
            if k == 0:
                place(turned.at[k], dst, send, recv, device_at(*turned_at, z, xl), turned_here, when)
            else:
                copy(turned.at[k], passing, send, u_recv, below, when)
            row_at = z3 if k else z
            copy(
                upright.at[k], upright_in.at[xl, yl], d_send.at[k], d_recv.at[2 * xl + yl],
                device_at(2 * xh + (row_at >> 1), 2 * yh + (row_at & 1), z + 1, c), when,
            )

    def pass_on(when):
        @pl.when(when)
        def _():
            wait_for(passing, u_recv)

        two = z ^ 2
        at_x, at_y = 2 * yh + (two >> 1), 2 * xh + (two & 1)
        here = (at_x == x) & (at_y == y) & (xl == c)
        place(
            passing, turned_in.at[c, yl], u_send, t_recv.at[2 * c + yl], device_at(at_x, at_y, z, xl), here, when
        )

    early_one(0, base, base.at[yh, c])

    @pl.loop(0, 4)
    def _(k):
        value = product(base, base.at[oh, c], k)
        late[0, k, 0] = value[:, :near]
        late[0, k, 1] = value[:, near:]

    send_late(0, 0)

    for k in range(2):
        wait_for(south.at[oh, c, :, pl.ds(k * near, near)], m_recv.at[1 + k])
    copy(south.at[oh, c], south.at[oh, c], ms_send.at[1], ms_recv.at[1], sibling)

    wait_for(north.at[yh], n_recv.at[0])
    early_one(1, base, north.at[yh])

    wait_for(south.at[yh, oc], ms_recv.at[0])
    wait_for(south.at[oh, oc], ms_recv.at[1])
    piece_rows = pl.ds(pl.multiple_of((z >> 1) * quarter, quarter), quarter)
    early_one(2, south, north.at[yh, piece_rows])

    early_two(0)

    early_two(1)
    early_two(2)

    for k in range(3):
        wait_for(late_in.at[0, k], h_recv.at[0, k, 0])
    late_two(0, 0)
    late_two(0, 1)

    for q in range(2):
        columns = pl.ds(q * near, near)
        for k in range(2):
            wait_for(north.at[(oh, *tile(2 * q + k))], n_recv.at[1 + 2 * q + k])
        late_one(1, base, north.at[oh, :, columns], q)
        late_one(2, south, north.at[oh, piece_rows, columns], q)
        if q == 0:
            late_two(1, 0)
            late_two(2, 0)

    for k in range(1, 8):
        rows = pl.ds(pl.multiple_of(((chip - k) & 7) * 8, 8), 8)
        wait_for(proj.at[c, rows], g_recv.at[k - 1])
    copy(proj.at[c], proj.at[c], f_send, f_recv, sibling)

    diag[...] = total(0)
    place(
        diag, diag_in.at[xl, yl], e_send, e_recv.at[2 * xl + yl], device_at(*diag_at, z, c), diag_here
    )

    deliver(yl == 0)
    wait_for(proj.at[oc], f_recv)
    sums = jnp.zeros((2 * rank, cols), F32)
    squares = jnp.zeros((rank, 1), F32)
    for k in range(2):
        value = proj[k]
        squares = squares + jnp.sum(value * value, axis=1, keepdims=True)
        sums = sums + jnp.dot(
            jnp.concatenate(split(value), axis=0), own[k * half : (k + 1) * half, :], preferred_element_type=F32
        )
    weight[:, :cols] = sums[:rank] + sums[rank:]
    weight[:, cols:] = jnp.broadcast_to(squares, (rank, 128))
    for k in range(1, 4):
        copy(weight, weights.at[k - 1], w_send.at[k - 1], w_recv.at[k - 1], device_at(x + k, y, z, c))

    late_two(1, 1)
    late_two(2, 1)
    pass_on(yl == 0)
    deliver(yl == 1)
    for k in range(3):
        wait_for(weights.at[k], w_recv.at[k])
    weight_sum[...] = (weight[...] + weights[0]) + (weights[1] + weights[2])
    copy(weight_sum, weights.at[3], w_send.at[3], w_recv.at[3], beside)
    pass_on(yl == 1)
    wait_for(weights.at[3], w_recv.at[3])
    both = weight_sum[...] + weights[3]
    scale = lax.rsqrt(both[:, cols : cols + 1] / total_cells)
    root = jnp.sqrt(jnp.float32(total_cells))
    amplitude = (root * (both[:, :cols] / total_cells)) * scale
    amps[...] = amplitude
    high, low = split(amplitude)

    for k in range(2):
        modes[:, k * half : (k + 1) * half] = (proj[k] * scale).astype(BF16)


    @pl.loop(0, 6)
    def _(k):
        at = pl.ds(pl.multiple_of(k * (cells // 6), cells // 6), cells // 6)
        block = modes[:, at]
        slow = lax.dot_general(block, high, (((0,), (0,)), ((), ())), preferred_element_type=F32)
        slow = slow + lax.dot_general(block, low, (((0,), (0,)), ((), ())), preferred_element_type=F32)
        resid[at, :] = (own[at, :].astype(F32) - slow / root).astype(BF16)


    @pl.when(role == 0)
    def _():
        for i in range(2):
            for j in range(2):
                wait_for(diag_in.at[i, j], e_recv.at[2 * i + j])
                gram[i * cols : (i + 1) * cols, j * near : (j + 1) * near] = diag_in[i, j]

    def block_of(tiles, recv, i, axis):
        for j in range(2):
            wait_for(tiles.at[i, j], recv.at[2 * i + j])
        return jnp.concatenate([tiles[i, 0], tiles[i, 1]], axis=axis).astype(F32)

    def upright_block(i):
        return block_of(upright_in, d_recv, i, 1)

    def turned_block(i):
        return block_of(turned_in, t_recv, i, 0)

    @pl.when(role == 1)
    def _():
        for i in range(2):
            gram[i * cols : (i + 1) * cols, :] = turned_block(i)

    @pl.when(role == 3)
    def _():
        for i in range(2):
            gram[i * cols : (i + 1) * cols, :] = upright_block(i)

    @pl.when(role == 2)
    def _():
        for i in range(2):
            gram[i * cols : (i + 1) * cols, :] = upright_block(i) + turned_block(i)

    for remote, when in pending:
        if when is None:
            remote.wait_send()
        else:
            pl.when(when)(remote.wait_send)


def hand_over(*refs):
    sources, targets, held, sems = refs[:4], refs[4:8], refs[8:12], refs[12]
    inward = [pltpu.make_async_copy(sources[k], held[k], sems.at[0, k]) for k in range(4)]
    outward = [pltpu.make_async_copy(held[k], targets[k], sems.at[1, k]) for k in range(4)]
    for one in inward:
        one.start()
    for first, then in zip(inward, outward):
        first.wait()
        then.start()
    for one in outward:
        one.wait()


def body(snapshots, coefficients):
    cells, cols = snapshots.shape
    snaps, rank = coefficients.shape
    half, quarter = cells // 2, cells // 4
    dma = pltpu.SemaphoreType.DMA
    rows, near = 2 * cols, cols // 2
    results = pl.pallas_call(
        kernel,
        out_shape=(
            jax.ShapeDtypeStruct((rows, cols), F32),
            jax.ShapeDtypeStruct((rank, cells), BF16),
            jax.ShapeDtypeStruct((rank, cols), F32),
            jax.ShapeDtypeStruct((cells, cols), BF16),
        ),
        in_specs=[pl.BlockSpec(memory_space=pl.ANY)] * 2,
        out_specs=[pl.BlockSpec(memory_space=pltpu.VMEM)] * 4,
        scratch_shapes=[
            pltpu.VMEM((cells, cols), BF16),
            pltpu.VMEM((rank, cols), BF16),
            pltpu.VMEM((2, 2, half, cols), BF16),
            pltpu.VMEM((2, half, cols), BF16),
            pltpu.VMEM((2, 2, quarter, cols), BF16),
            pltpu.VMEM((3, 2, 4, cols, near), BF16),
            pltpu.VMEM((3, 4, cols, near), BF16),
            pltpu.VMEM((3, 4, cols, near), BF16),
            pltpu.VMEM((3, 3, cols, near), BF16),
            pltpu.VMEM((3, 4, 2, cols, near), BF16),
            pltpu.VMEM((3, 3, 2, cols, near), BF16),
            pltpu.VMEM((3, 2, cols, near), BF16),
            pltpu.VMEM((3, 2, cols, near), BF16),
            pltpu.VMEM((cols, near), F32),
            pltpu.VMEM((2, 2, cols, near), F32),
            pltpu.VMEM((2, cols, near), BF16),
            pltpu.VMEM((2, 2, cols, near), BF16),
            pltpu.VMEM((2, near, cols), BF16),
            pltpu.VMEM((2, 2, near, cols), BF16),
            pltpu.VMEM((near, cols), BF16),
            pltpu.VMEM((rank, cells), F32),
            pltpu.VMEM((rank, half), F32),
            pltpu.VMEM((7, 8, half), F32),
            pltpu.VMEM((2, rank, half), F32),
            pltpu.VMEM((rank, cols + 128), F32),
            pltpu.VMEM((4, rank, cols + 128), F32),
            pltpu.VMEM((rank, cols + 128), F32),
            dma((3,)),
            dma((CHUNKS,)), dma((CHUNKS,)),
            dma((1 + CHUNKS,)), dma((1 + CHUNKS,)),
            dma((1 + CHUNKS,)), dma((1 + CHUNKS,)),
            dma((3,)), dma((3,)),
            dma((2,)), dma((2,)),
            dma((3,)), dma((3,)),
            dma((3, 3)), dma((3, 3)),
            dma((3, 3, 2)), dma((3, 3, 2)),
            dma((3, 2)), dma((3, 2)),
            dma, dma((4,)),
            dma((2,)), dma((4,)),
            dma((2,)), dma((4,)),
            dma, dma,
            dma, dma,
            dma((7,)), dma((7,)),
            dma((7,)), dma((7,)),
            dma, dma,
            dma((4,)), dma((4,)),
        ],
        compiler_params=pltpu.CompilerParams(
            collective_id=0, has_side_effects=True, vmem_limit_bytes=56 << 20
        ),
    )(snapshots, coefficients.T)
    gram, modes, amps, resid = pl.pallas_call(
        hand_over,
        out_shape=tuple(jax.ShapeDtypeStruct(r.shape, r.dtype) for r in results),
        in_specs=[pl.BlockSpec(memory_space=pl.ANY)] * 4,
        out_specs=[pl.BlockSpec(memory_space=pl.ANY)] * 4,
        scratch_shapes=[*(pltpu.VMEM(r.shape, r.dtype) for r in results), dma((2, 4))],
    )(*results)
    return gram, modes.T, amps.T, resid


def solution(mesh):
    return jax.shard_map(
        body,
        mesh=mesh,
        in_specs=(P("space", "tm"), P()),
        out_specs=(P("space", "tm"), P("space", None), P("tm", None), P("space", "tm")),
        check_vma=False,
    )
```

```python
import jax
import jax.numpy as jnp
from jax import lax
from jax.experimental import pallas as pl
from jax.experimental.pallas import tpu as pltpu
from jax.sharding import PartitionSpec as P

MESH = pl.DeviceIdType.MESH
F32, BF16 = jnp.float32, jnp.bfloat16
CHUNKS = 4


def device_at(x, y, z, c):
    x, y, z = x & 3, y & 3, z & 3
    return (x * 2 + (y & 1), (y >> 1) * 8 + z * 2 + c)


def wait_for(ref, sem):
    pltpu.make_async_copy(ref, ref, sem).wait()


def split(value):
    high = value.astype(BF16)
    return high, (value - high.astype(F32)).astype(BF16)


def kernel(
    snaps, coeffs, gram, modes, amps, resid,
    own, coef, base, north, south,
    early, early_in, early_sum, early_x, late, late_in, late_sum, late_y,
    diag, diag_in, upright, upright_in, turned, turned_in, passing,
    part, sib_part, pieces, proj, weight, weights, weight_sum,
    local_sem, y_send, y_recv, sib_send, sib_recv, n_send, n_recv, m_send, m_recv, ms_send, ms_recv,
    a_send, a_recv, b_send, b_recv, h_send, h_recv, l_send, l_recv,
    e_send, e_recv, d_send, d_recv, t_send, t_recv, u_send, u_recv,
    p_send, p_recv, r_send, r_recv, g_send, g_recv, f_send, f_recv, w_send, w_recv,
):
    space, tm = lax.axis_index("space"), lax.axis_index("tm")
    x, yl, yh, z, c = space >> 1, space & 1, tm >> 3, (tm >> 1) & 3, tm & 1
    y, chip, oh, ol, oc = 2 * yh + yl, tm >> 1, 1 - yh, 1 - yl, 1 - c
    xh, xl = x >> 1, x & 1
    cells, cols = own.shape
    half, quarter, near = cells // 2, cells // 4, cols // 2
    total_cells = cells * 8
    rank = coef.shape[0]
    role = (2 * xl + yl - z) & 3
    pending = []

    def copy(src, dst, send, recv, device, when=None):
        remote = pltpu.make_async_remote_copy(
            src_ref=src, dst_ref=dst, send_sem=send, recv_sem=recv, device_id=device, device_id_type=MESH
        )
        if when is None:
            remote.start()
        else:
            pl.when(when)(remote.start)
        pending.append((remote, when))

    def place(src, dst, send, recv, device, here, when=True):
        copy(src, dst, send, recv, device, jnp.logical_not(here) & when)
        pl.when(here & when)(pltpu.make_async_copy(src, dst, recv).start)

    sibling = device_at(x, y, z, oc)
    partner = device_at(x, y + 2, z, c)
    beside = device_at(x, 2 * yh + ol, z, c)
    across = device_at(x, 2 * oh + ol, z, c)
    below, above = device_at(x, y, z + 3, c), device_at(x, y, z + 1, c)

    z1, z3 = (z + 1) & 3, (z + 3) & 3
    diag_at = (2 * xh + (z >> 1), 2 * yh + (z & 1))
    diag_here = (xl == (z >> 1)) & (yl == (z & 1))
    turned_at = (2 * yh + (z1 >> 1), 2 * xh + (z1 & 1))
    turned_here = (turned_at[0] == x) & (turned_at[1] == y) & (xl == c)

    barrier = pltpu.get_barrier_semaphore()

    def greet(device, when=None):
        def do():
            pl.semaphore_signal(barrier, inc=1, device_id=device, device_id_type=MESH)

        do() if when is None else pl.when(when)(do)

    for device in (sibling, beside):
        greet(device)
    for k in range(1, 8):
        greet((space, ((chip + k) & 7) * 2 + c))
    for k in range(1, 4):
        greet(device_at(x + k, y, z, c))

    keep = pl.ds(pl.multiple_of(yh * half, half), half)
    mine = pltpu.make_async_copy(snaps.at[keep], base.at[yh, c], local_sem.at[0])
    whole = pltpu.make_async_copy(snaps, own, local_sem.at[1])
    coef_own = pltpu.make_async_copy(
        coeffs.at[:, pl.ds(pl.multiple_of(tm * cols, cols), cols)], coef, local_sem.at[2]
    )
    coef_own.start()
    whole.start()
    mine.start()
    pl.semaphore_wait(barrier, 12)

    for k in range(CHUNKS):
        rows = pl.ds(pl.multiple_of(oh * half + (k & 1) * quarter, quarter), quarter)
        columns = pl.ds((k >> 1) * near, near)
        copy(
            snaps.at[rows, columns], base.at[yh, c, pl.ds((k & 1) * quarter, quarter), columns],
            y_send.at[k], y_recv.at[k], partner,
        )
    copy(snaps.at[keep], base.at[yh, c], sib_send.at[0], sib_recv.at[0], sibling)
    copy(snaps.at[keep], north.at[yh], n_send.at[0], n_recv.at[0], below)
    piece_for = z1 >> 1
    rows = pl.ds(pl.multiple_of(yh * half + piece_for * quarter, quarter), quarter)
    copy(snaps.at[rows], south.at[yh, c], m_send.at[0], m_recv.at[0], above)

    coef_own.wait()
    whole.wait()
    part[...] = lax.dot_general(coef[...], own[...], (((1,), (1,)), ((), ())), preferred_element_type=F32)
    other_half = pl.ds(pl.multiple_of(oc * half, half), half)
    copy(part.at[:, other_half], sib_part, p_send, p_recv, sibling)
    wait_for(sib_part, p_recv)
    own_half = pl.ds(pl.multiple_of(c * half, half), half)
    sib_part[...] += part[:, own_half]
    for k in range(1, 8):
        to = (chip + k) & 7
        rows = pl.ds(pl.multiple_of(to * 8, 8), 8)
        copy(sib_part.at[rows], pieces.at[k - 1], r_send.at[k - 1], r_recv.at[k - 1], (space, to * 2 + c))

    def tile(k):
        return pl.ds((k & 1) * quarter, quarter), pl.ds((k >> 1) * near, near)

    def relay(k):
        rows, columns = tile(k)
        src = base.at[oh, c, rows, columns]
        wait_for(src, y_recv.at[k])
        copy(src, src, sib_send.at[1 + k], sib_recv.at[1 + k], sibling)
        copy(src, north.at[oh, rows, columns], n_send.at[1 + k], n_recv.at[1 + k], below)
        copy(
            src, south.at[oh, c, :, columns], m_send.at[1 + (k >> 1)], m_recv.at[1 + (k >> 1)], above,
            piece_for == (k & 1),
        )

    relay(0)
    relay(1)
    relay(2)
    relay(3)

    for k in range(7):
        wait_for(pieces.at[k], r_recv.at[k])
    rows8 = pl.ds(pl.multiple_of(chip * 8, 8), 8)
    piece = sib_part[rows8, :]
    for k in range(7):
        piece = piece + pieces[k]
    proj[c, rows8, :] = piece
    for k in range(1, 8):
        to = (chip + k) & 7
        copy(proj.at[c, rows8], proj.at[c, rows8], g_send.at[k - 1], g_recv.at[k - 1], (space, to * 2 + c))

    mine.wait()

    wait_for(south.at[yh, c], m_recv.at[0])
    copy(south.at[yh, c], south.at[yh, c], ms_send.at[0], ms_recv.at[0], sibling)

    wait_for(base.at[yh, oc], sib_recv.at[0])
    for k in range(CHUNKS):
        wait_for(base.at[(oh, oc, *tile(k))], sib_recv.at[1 + k])

    def product(left, right, k):
        return lax.dot_general(
            left[k // 2, k % 2], right[...], (((0,), (0,)), ((), ())), preferred_element_type=F32
        ).astype(BF16)

    def early_one(kind, left, right):
        @pl.loop(0, 4)
        def _(k):
            value = product(left, right, k)
            early[kind, 0, k] = value[:, : cols // 2]
            early[kind, 1, k] = value[:, cols // 2 :]

        copy(early.at[kind, ol], early_in.at[kind], a_send.at[kind], a_recv.at[kind], beside)

    def early_two(kind):
        wait_for(early_in.at[kind], a_recv.at[kind])
        early_sum[kind] = (early[kind, yl].astype(F32) + early_in[kind].astype(F32)).astype(BF16)
        for k in range(1, 4):
            copy(
                early_sum.at[kind, (x + k) & 3], early_x.at[kind, k - 1],
                b_send.at[kind, k - 1], b_recv.at[kind, k - 1], device_at(x + k, y, z, c),
            )

    def send_late(kind, q):
        for k in range(1, 4):
            to = (x + k) & 3
            src, dst = late.at[kind, to], late_in.at[kind, k - 1]
            if kind:
                src, dst = src.at[q], dst.at[q]
            copy(src, dst, h_send.at[kind, k - 1, q], h_recv.at[kind, k - 1, q], device_at(x + k, y, z, c))

    def late_one(kind, left, right, q):
        @pl.loop(0, 4)
        def _(k):
            late[kind, k, q] = product(left, right, k)

        send_late(kind, q)

    def late_two(kind, q):
        value = late[kind, x, q].astype(F32)
        for k in range(3):
            if kind:
                wait_for(late_in.at[kind, k, q], h_recv.at[kind, k, q])
            value = value + late_in[kind, k, q].astype(F32)
        late_sum[kind, q] = value.astype(BF16)
        copy(
            late_sum.at[kind, q], late_y.at[kind, yl ^ q], l_send.at[kind, q], l_recv.at[kind, yl ^ q],
            device_at(x, 2 * oh + q, z, c),
        )

    def total(kind):
        value = early_sum[kind, x].astype(F32)
        for k in range(3):
            wait_for(early_x.at[kind, k], b_recv.at[kind, k])
            value = value + early_x[kind, k].astype(F32)
        for k in range(2):
            wait_for(late_y.at[kind, k], l_recv.at[kind, k])
            value = value + late_y[kind, k].astype(F32)
        return value / total_cells

    def deliver(when):
        @pl.when(when)
        def _():
            for k in range(2):
                value = total(k + 1)
                upright[k] = value.astype(BF16)
                turned[k] = value.T.astype(BF16)

        for k in range(2):
            dst, send, recv = turned_in.at[c, yl], t_send.at[k], t_recv.at[2 * c + yl]
            if k == 0:
                place(turned.at[k], dst, send, recv, device_at(*turned_at, z, xl), turned_here, when)
            else:
                copy(turned.at[k], passing, send, u_recv, below, when)
            row_at = z3 if k else z
            copy(
                upright.at[k], upright_in.at[xl, yl], d_send.at[k], d_recv.at[2 * xl + yl],
                device_at(2 * xh + (row_at >> 1), 2 * yh + (row_at & 1), z + 1, c), when,
            )

    def pass_on(when):
        @pl.when(when)
        def _():
            wait_for(passing, u_recv)

        two = z ^ 2
        at_x, at_y = 2 * yh + (two >> 1), 2 * xh + (two & 1)
        here = (at_x == x) & (at_y == y) & (xl == c)
        place(
            passing, turned_in.at[c, yl], u_send, t_recv.at[2 * c + yl], device_at(at_x, at_y, z, xl), here, when
        )

    early_one(0, base, base.at[yh, c])

    @pl.loop(0, 4)
    def _(k):
        value = product(base, base.at[oh, c], k)
        late[0, k, 0] = value[:, :near]
        late[0, k, 1] = value[:, near:]

    send_late(0, 0)

    for k in range(2):
        wait_for(south.at[oh, c, :, pl.ds(k * near, near)], m_recv.at[1 + k])
    copy(south.at[oh, c], south.at[oh, c], ms_send.at[1], ms_recv.at[1], sibling)

    wait_for(north.at[yh], n_recv.at[0])
    early_one(1, base, north.at[yh])

    wait_for(south.at[yh, oc], ms_recv.at[0])
    wait_for(south.at[oh, oc], ms_recv.at[1])
    piece_rows = pl.ds(pl.multiple_of((z >> 1) * quarter, quarter), quarter)
    early_one(2, south, north.at[yh, piece_rows])

    early_two(0)

    early_two(1)
    early_two(2)

    for k in range(3):
        wait_for(late_in.at[0, k], h_recv.at[0, k, 0])
    late_two(0, 0)
    late_two(0, 1)

    for q in range(2):
        columns = pl.ds(q * near, near)
        for k in range(2):
            wait_for(north.at[(oh, *tile(2 * q + k))], n_recv.at[1 + 2 * q + k])
        late_one(1, base, north.at[oh, :, columns], q)
        late_one(2, south, north.at[oh, piece_rows, columns], q)
        if q == 0:
            late_two(1, 0)
            late_two(2, 0)

    for k in range(1, 8):
        rows = pl.ds(pl.multiple_of(((chip - k) & 7) * 8, 8), 8)
        wait_for(proj.at[c, rows], g_recv.at[k - 1])
    copy(proj.at[c], proj.at[c], f_send, f_recv, sibling)

    diag[...] = total(0)
    place(
        diag, diag_in.at[xl, yl], e_send, e_recv.at[2 * xl + yl], device_at(*diag_at, z, c), diag_here
    )

    deliver(yl == 0)
    wait_for(proj.at[oc], f_recv)
    sums = jnp.zeros((2 * rank, cols), F32)
    squares = jnp.zeros((rank, 1), F32)
    for k in range(2):
        value = proj[k]
        squares = squares + jnp.sum(value * value, axis=1, keepdims=True)
        sums = sums + jnp.dot(
            jnp.concatenate(split(value), axis=0), own[k * half : (k + 1) * half, :], preferred_element_type=F32
        )
    weight[:, :cols] = sums[:rank] + sums[rank:]
    weight[:, cols:] = jnp.broadcast_to(squares, (rank, 128))
    for k in range(1, 4):
        copy(weight, weights.at[k - 1], w_send.at[k - 1], w_recv.at[k - 1], device_at(x + k, y, z, c))

    late_two(1, 1)
    late_two(2, 1)
    pass_on(yl == 0)
    deliver(yl == 1)
    for k in range(3):
        wait_for(weights.at[k], w_recv.at[k])
    weight_sum[...] = (weight[...] + weights[0]) + (weights[1] + weights[2])
    copy(weight_sum, weights.at[3], w_send.at[3], w_recv.at[3], beside)
    pass_on(yl == 1)
    wait_for(weights.at[3], w_recv.at[3])
    both = weight_sum[...] + weights[3]
    scale = lax.rsqrt(both[:, cols : cols + 1] / total_cells)
    root = jnp.sqrt(jnp.float32(total_cells))
    amplitude = (root * (both[:, :cols] / total_cells)) * scale
    amps[...] = amplitude
    high, low = split(amplitude)

    for k in range(2):
        modes[:, k * half : (k + 1) * half] = (proj[k] * scale).astype(BF16)


    @pl.loop(0, 6)
    def _(k):
        at = pl.ds(pl.multiple_of(k * (cells // 6), cells // 6), cells // 6)
        block = modes[:, at]
        slow = lax.dot_general(block, high, (((0,), (0,)), ((), ())), preferred_element_type=F32)
        slow = slow + lax.dot_general(block, low, (((0,), (0,)), ((), ())), preferred_element_type=F32)
        resid[at, :] = (own[at, :].astype(F32) - slow / root).astype(BF16)


    @pl.when(role == 0)
    def _():
        for i in range(2):
            for j in range(2):
                wait_for(diag_in.at[i, j], e_recv.at[2 * i + j])
                gram[i * cols : (i + 1) * cols, j * near : (j + 1) * near] = diag_in[i, j]

    def block_of(tiles, recv, i, axis):
        for j in range(2):
            wait_for(tiles.at[i, j], recv.at[2 * i + j])
        return jnp.concatenate([tiles[i, 0], tiles[i, 1]], axis=axis).astype(F32)

    def upright_block(i):
        return block_of(upright_in, d_recv, i, 1)

    def turned_block(i):
        return block_of(turned_in, t_recv, i, 0)

    @pl.when(role == 1)
    def _():
        for i in range(2):
            gram[i * cols : (i + 1) * cols, :] = turned_block(i)

    @pl.when(role == 3)
    def _():
        for i in range(2):
            gram[i * cols : (i + 1) * cols, :] = upright_block(i)

    @pl.when(role == 2)
    def _():
        for i in range(2):
            gram[i * cols : (i + 1) * cols, :] = upright_block(i) + turned_block(i)

    for remote, when in pending:
        if when is None:
            remote.wait_send()
        else:
            pl.when(when)(remote.wait_send)


def hand_over(*refs):
    sources, targets, held, sems = refs[:4], refs[4:8], refs[8:12], refs[12]
    parts = [(k, i) for i in range(4) for k in (3, 0, 1, 2)]

    def part_of(ref, i):
        rows = ref.shape[0] // 4
        return ref.at[pl.ds(i * rows, rows)]

    inward, outward = [], []
    for k, i in parts:
        slot = part_of(held[k], i)
        inward.append(pltpu.make_async_copy(part_of(sources[k], i), slot, sems.at[0, k, i]))
        outward.append(pltpu.make_async_copy(slot, part_of(targets[k], i), sems.at[1, k, i]))
    for one in inward:
        one.start()
    for first, then in zip(inward, outward):
        first.wait()
        then.start()
    for one in outward:
        one.wait()


def body(snapshots, coefficients):
    cells, cols = snapshots.shape
    snaps, rank = coefficients.shape
    half, quarter = cells // 2, cells // 4
    dma = pltpu.SemaphoreType.DMA
    rows, near = 2 * cols, cols // 2
    results = pl.pallas_call(
        kernel,
        out_shape=(
            jax.ShapeDtypeStruct((rows, cols), F32),
            jax.ShapeDtypeStruct((rank, cells), BF16),
            jax.ShapeDtypeStruct((rank, cols), F32),
            jax.ShapeDtypeStruct((cells, cols), BF16),
        ),
        in_specs=[pl.BlockSpec(memory_space=pl.ANY)] * 2,
        out_specs=[pl.BlockSpec(memory_space=pltpu.VMEM)] * 4,
        scratch_shapes=[
            pltpu.VMEM((cells, cols), BF16),
            pltpu.VMEM((rank, cols), BF16),
            pltpu.VMEM((2, 2, half, cols), BF16),
            pltpu.VMEM((2, half, cols), BF16),
            pltpu.VMEM((2, 2, quarter, cols), BF16),
            pltpu.VMEM((3, 2, 4, cols, near), BF16),
            pltpu.VMEM((3, 4, cols, near), BF16),
            pltpu.VMEM((3, 4, cols, near), BF16),
            pltpu.VMEM((3, 3, cols, near), BF16),
            pltpu.VMEM((3, 4, 2, cols, near), BF16),
            pltpu.VMEM((3, 3, 2, cols, near), BF16),
            pltpu.VMEM((3, 2, cols, near), BF16),
            pltpu.VMEM((3, 2, cols, near), BF16),
            pltpu.VMEM((cols, near), F32),
            pltpu.VMEM((2, 2, cols, near), F32),
            pltpu.VMEM((2, cols, near), BF16),
            pltpu.VMEM((2, 2, cols, near), BF16),
            pltpu.VMEM((2, near, cols), BF16),
            pltpu.VMEM((2, 2, near, cols), BF16),
            pltpu.VMEM((near, cols), BF16),
            pltpu.VMEM((rank, cells), F32),
            pltpu.VMEM((rank, half), F32),
            pltpu.VMEM((7, 8, half), F32),
            pltpu.VMEM((2, rank, half), F32),
            pltpu.VMEM((rank, cols + 128), F32),
            pltpu.VMEM((4, rank, cols + 128), F32),
            pltpu.VMEM((rank, cols + 128), F32),
            dma((3,)),
            dma((CHUNKS,)), dma((CHUNKS,)),
            dma((1 + CHUNKS,)), dma((1 + CHUNKS,)),
            dma((1 + CHUNKS,)), dma((1 + CHUNKS,)),
            dma((3,)), dma((3,)),
            dma((2,)), dma((2,)),
            dma((3,)), dma((3,)),
            dma((3, 3)), dma((3, 3)),
            dma((3, 3, 2)), dma((3, 3, 2)),
            dma((3, 2)), dma((3, 2)),
            dma, dma((4,)),
            dma((2,)), dma((4,)),
            dma((2,)), dma((4,)),
            dma, dma,
            dma, dma,
            dma((7,)), dma((7,)),
            dma((7,)), dma((7,)),
            dma, dma,
            dma((4,)), dma((4,)),
        ],
        compiler_params=pltpu.CompilerParams(
            collective_id=0, has_side_effects=True, vmem_limit_bytes=56 << 20
        ),
    )(snapshots, coefficients.T)
    gram, modes, amps, resid = pl.pallas_call(
        hand_over,
        out_shape=tuple(jax.ShapeDtypeStruct(r.shape, r.dtype) for r in results),
        in_specs=[pl.BlockSpec(memory_space=pl.ANY)] * 4,
        out_specs=[pl.BlockSpec(memory_space=pl.ANY)] * 4,
        scratch_shapes=[*(pltpu.VMEM(r.shape, r.dtype) for r in results), dma((2, 4, 4))],
    )(*results)
    return gram, modes.T, amps.T, resid


def solution(mesh):
    return jax.shard_map(
        body,
        mesh=mesh,
        in_specs=(P("space", "tm"), P()),
        out_specs=(P("space", "tm"), P("space", None), P("tm", None), P("space", "tm")),
        check_vma=False,
    )
```
